128 devices in a mesh: mem: 16 (over z, x), slab: 8 (over y, core).
Axes of the slice: x: 4, y: 4, z: 4, core: 2. Of those that a mesh axis runs over, the one named last changes fastest.
Arguments:
- pressure: float32 [128, 256, 4096], P('mem', 'slab'), may hold values from 0.5 to 3
- content: float32 [128, 256, 4096], P('mem', 'slab'), may hold values from 0.5 to 3
- diffusivity: float32 [256, 4096], P('slab'), may hold values from 0.05 to 1
- langmuir_pressure: float32 [256, 4096], P('slab'), may hold values from 0.5 to 4
- langmuir_volume: float32 [256, 4096], P('slab'), may hold values from 1 to 3
- desorb_rate: float32 [256, 4096], P('slab'), may hold values from 0.02 to 0.5
- observed_cell: int32 [64, 128, 16], P('slab', 'mem'), may hold values from 0 to 127
- observed_value: float32 [64, 128, 16], P('slab', 'mem'), may hold values from 0.5 to 3.5
- error_weight: float32 [64, 128, 16], P('slab', 'mem'), may hold values from 0.25 to 2.5
- observed_count: int32 [64, 128], P('slab', 'mem'), may hold values from 1 to 16, as said below
- neighbour: int32 [64, 128, 4], P('slab', 'mem'), may hold values from 0 to 8, as said below
Outputs:
- analysis: float32 [128, 256, 4096], P(None, 'slab', 'mem')
- gas_content: float32 [128, 256, 4096], P('mem', 'slab')
The draws below stay inside these ranges and needn't reach their ends.
Inputs may be any that keep to these rules, and one draw needn't show every extreme that they name: `observed_cell`: the slot's cell within its block, row * 32 + column. Some block has 16 live slots and some block has 1; slots j < observed_count are live. `neighbour`: A block's 4 codes are distinct; code q names the block (q // 3 - 1, q % 3 - 1) away, 4 the block itself.
All inputs are finite; a program needn't handle non-finite values.
Results may differ from the reference program's by a relative error of at most 0.0001.
Values sent between devices are 32-bit elements; how exact they have to be, the bound alone decides.
A program may use at most 192 MiB of HBM per device.

```python
import math
import jax
import jax.numpy as jnp
from jax import lax

MEMBERS = 128
NX = 256
NY = 4096
STEPS = 4
BR = 4
BC = 32
OBS_MAX = 16
NBR = 4
NS_ITERS = 7
NBX = 64
NBY = 128


def draw_pressure(key, part):
    key = jax.random.fold_in(key, 10)
    member_key = jax.random.fold_in(key, 1)
    cell_key = jax.random.fold_in(key, 2)
    offset = jnp.clip(0.6 * jax.random.normal(member_key, (MEMBERS, 1, 1), jnp.float32), -1.0, 1.0)
    noise = jax.random.uniform(cell_key, (MEMBERS, NX, NY), jnp.float32, -1.0, 1.0)
    return (1.75 + 0.9 * offset + 0.35 * noise).astype(jnp.float32)


def draw_observed_count(key, part):
    key = jax.random.fold_in(key, 11)
    raw = jax.random.randint(key, (NBX, NBY), 0, OBS_MAX)
    counts = 1 + raw
    counts = counts.at[0, 0].set(OBS_MAX)
    counts = counts.at[0, 1].set(1)
    return counts.astype(jnp.int32)


def draw_neighbour(key, part):
    key = jax.random.fold_in(key, 12)
    scores = jax.random.randint(key, (NBX, NBY, 9), 0, 1 << 20) * 16 + jnp.arange(9, dtype=jnp.int32)
    order = jnp.argsort(scores, axis=-1, stable=True)
    return order[..., :NBR].astype(jnp.int32)


def plant(array, stream_key, low, top_value):
    longest = array.shape.index(max(array.shape))
    spots = []
    for shift in (0, 1):
        where = [jax.random.randint(jax.random.fold_in(stream_key, axis), (), 0, length) for axis, length in enumerate(array.shape)]
        where[longest] = (where[longest] + shift) % array.shape[longest]
        spots.append(tuple(where))
    return array.at[spots[0]].set(low).at[spots[1]].set(top_value)


def shard_levels(stream_key, extent, shards, smallest, high):
    level = 1.0
    for dim, shards_of in shards:
        draws = jax.random.uniform(jax.random.fold_in(jax.random.fold_in(stream_key, 6), dim), (shards_of,), jnp.float32, smallest / len(shards), high / len(shards))
        level = level * jnp.repeat(jnp.exp(draws), extent[dim] // shards_of).reshape((-1,) + (1,) * (len(extent) - 1 - dim))
    return level


def setup_inputs(seed: int = 0) -> dict:
    key_of = jax.random.split(jax.random.key(seed), 12)
    pressure = draw_pressure(jax.random.fold_in(key_of[11], 71), 0)
    content = jnp.clip(0.5 + 2.5 * jax.random.uniform(key_of[1], (MEMBERS, NX, NY), jnp.float32) ** shard_levels(key_of[1], (MEMBERS, NX, NY), ((0, 16), (1, 8)), -0.2, 0.2), 0.5, 3.0)
    diffusivity = jnp.clip(jnp.exp(math.log(1.0) - 2.9957323 * jax.random.uniform(key_of[2], (NX, NY), jnp.float32) ** shard_levels(key_of[2], (NX, NY), ((0, 8),), -0.2, 0.2)), 0.05, 1.0)
    langmuir_pressure = jnp.clip(jnp.exp(math.log(4.0) - 2.0794415 * jax.random.uniform(key_of[3], (NX, NY), jnp.float32) ** shard_levels(key_of[3], (NX, NY), ((0, 8),), -0.2, 0.2)), 0.5, 4.0)
    langmuir_volume = jnp.clip(jnp.exp(math.log(3.0) - 1.0986123 * jax.random.uniform(key_of[4], (NX, NY), jnp.float32) ** shard_levels(key_of[4], (NX, NY), ((0, 8),), -0.2, 0.2)), 1.0, 3.0)
    desorb_rate = jnp.clip(jnp.exp(math.log(0.5) - 3.218876 * jax.random.uniform(key_of[5], (NX, NY), jnp.float32) ** shard_levels(key_of[5], (NX, NY), ((0, 8),), -0.2, 0.2)), 0.02, 0.5)
    observed_cell = plant(jax.random.randint(key_of[6], (NBX, NBY, OBS_MAX), 0, BR * BC), jax.random.fold_in(key_of[6], 1), 0, (BR * BC) - 1).astype(jnp.int32)
    observed_value = jnp.clip(0.5 + 3.0 * jax.random.uniform(key_of[7], (NBX, NBY, OBS_MAX), jnp.float32) ** shard_levels(key_of[7], (NBX, NBY, OBS_MAX), ((0, 8), (1, 16)), -0.2, 0.2), 0.5, 3.5)
    error_weight = jnp.clip(jnp.exp(math.log(2.5) - 2.3025851 * jax.random.uniform(key_of[8], (NBX, NBY, OBS_MAX), jnp.float32) ** shard_levels(key_of[8], (NBX, NBY, OBS_MAX), ((0, 8), (1, 16)), -0.2, 0.2)), 0.25, 2.5)
    observed_count = draw_observed_count(jax.random.fold_in(key_of[11], 71), 0)
    neighbour = draw_neighbour(jax.random.fold_in(key_of[11], 71), 0)
    return {"pressure": pressure, "content": content, "diffusivity": diffusivity, "langmuir_pressure": langmuir_pressure, "langmuir_volume": langmuir_volume, "desorb_rate": desorb_rate, "observed_cell": observed_cell, "observed_value": observed_value, "error_weight": error_weight, "observed_count": observed_count, "neighbour": neighbour}


time_step = 0.2
inflation = 1.1
highest = lax.Precision.HIGHEST
root_weight = [math.exp(-0.25 * ((index // 3 - 1) ** 2 + (index % 3 - 1) ** 2)) for index in range(9)]

def diffuse(pressure_pad, conduct_pad, content_now, desorb_rate, langmuir_pressure, langmuir_volume):
    middle = pressure_pad[:, 1:-1]
    conduct = conduct_pad[1:-1]
    side_field = jnp.pad(middle, ((0, 0), (0, 0), (1, 1)))
    side_conduct = jnp.pad(conduct, ((0, 0), (1, 1)))
    net_flow = 0.5 * (conduct + conduct_pad[:-2]) * (pressure_pad[:, :-2] - middle)
    net_flow = net_flow + 0.5 * (conduct + conduct_pad[2:]) * (pressure_pad[:, 2:] - middle)
    net_flow = net_flow + 0.5 * (conduct + side_conduct[:, :-2]) * (side_field[:, :, :-2] - middle)
    net_flow = net_flow + 0.5 * (conduct + side_conduct[:, 2:]) * (side_field[:, :, 2:] - middle)
    sorbed = langmuir_volume * middle / (langmuir_pressure + jnp.abs(middle))
    release = desorb_rate * (content_now - sorbed)
    return (middle + time_step * net_flow + release, content_now - release)

def to_blocks(field):
    leading, row_count, col_count = field.shape
    shaped = field.reshape(leading, row_count // BR, BR, col_count // BC, BC)
    return shaped.transpose(1, 3, 0, 2, 4).reshape(row_count // BR, col_count // BC, leading, BR * BC)

def from_blocks(blocks):
    count_x, count_y, leading, cells = blocks.shape
    shaped = blocks.reshape(count_x, count_y, leading, BR, BC)
    return shaped.transpose(2, 0, 3, 1, 4).reshape(leading, count_x * BR, count_y * BC)

def observe(mean_blocks, dev_blocks, observed_cell, observed_value, error_weight, observed_count):
    onehot = (observed_cell[..., None] == jnp.arange(BR * BC, dtype=jnp.int32)[None, None, None, :]).astype(jnp.float32)
    spread = jnp.einsum('abjc,abmc->abjm', onehot, dev_blocks, precision=highest)
    centre = jnp.einsum('abjc,abc->abj', onehot, mean_blocks[:, :, 0], precision=highest)
    live_mask = (jnp.arange(OBS_MAX, dtype=jnp.int32)[None, None, :] < observed_count[..., None]).astype(jnp.float32)
    root_error = jnp.sqrt(error_weight) * live_mask
    scaled = spread * root_error[..., None]
    innovation = (observed_value - centre) * root_error
    row_pad = jnp.pad(innovation, ((0, 0), (0, 0), (0, MEMBERS - OBS_MAX)))
    return jnp.concatenate([scaled, row_pad[:, :, None, :]], axis=2)

def select(padded, neighbour):
    count_x, count_y = (neighbour.shape[0], neighbour.shape[1])
    chosen = jnp.zeros((count_x, count_y, NBR, OBS_MAX + 1, MEMBERS), jnp.float32)
    for offset_code in range(9):
        shift_x = offset_code // 3
        shift_y = offset_code % 3
        window = padded[shift_x:shift_x + count_x, shift_y:shift_y + count_y]
        weight = (neighbour == offset_code).astype(jnp.float32) * root_weight[offset_code]
        chosen = chosen + weight[..., None, None] * window[:, :, None]
    local_obs = chosen[:, :, :, :OBS_MAX, :].reshape(count_x, count_y, NBR * OBS_MAX, MEMBERS)
    local_innov = chosen[:, :, :, OBS_MAX, :OBS_MAX].reshape(count_x, count_y, NBR * OBS_MAX)
    return (local_obs, local_innov)

def analyze(mean_blocks, dev_blocks, local_obs, local_innov):
    gram_matrix = jnp.einsum('abom,abon->abmn', local_obs, local_obs, precision=highest)
    pull_vector = jnp.einsum('abo,abom->abm', local_innov, local_obs, precision=highest)
    identity = jnp.eye(MEMBERS, dtype=jnp.float32)
    system = gram_matrix + (MEMBERS - 1) / inflation * identity
    trace_bound = jnp.trace(system, axis1=2, axis2=3)
    root_now = system / trace_bound[..., None, None]
    inverse_root = jnp.broadcast_to(identity, system.shape)
    for sweep_index in range(NS_ITERS):
        product = jnp.einsum('abij,abjk->abik', inverse_root, root_now, precision=highest)
        factor = 0.5 * (3.0 * identity - product)
        root_now = jnp.einsum('abij,abjk->abik', root_now, factor, precision=highest)
        inverse_root = jnp.einsum('abij,abjk->abik', factor, inverse_root, precision=highest)
    inverse_root = inverse_root / jnp.sqrt(trace_bound)[..., None, None]
    first_pass = jnp.einsum('abij,abj->abi', inverse_root, pull_vector, precision=highest)
    shift_mean = jnp.einsum('abij,abj->abi', inverse_root, first_pass, precision=highest)
    weights = math.sqrt(MEMBERS - 1) * inverse_root + shift_mean[..., :, None]
    return mean_blocks + jnp.einsum('abji,abjc->abic', weights, dev_blocks, precision=highest)

def reference(pressure, content, diffusivity, langmuir_pressure, langmuir_volume, desorb_rate, observed_cell, observed_value, error_weight, observed_count, neighbour):
    pressure_now, content_now = (pressure, content)
    conduct_pad = jnp.pad(diffusivity, ((1, 1), (0, 0)))
    for step_index in range(STEPS):
        pressure_pad = jnp.pad(pressure_now, ((0, 0), (1, 1), (0, 0)))
        pressure_now, content_now = diffuse(pressure_pad, conduct_pad, content_now, desorb_rate, langmuir_pressure, langmuir_volume)
    centre_field = lax.optimization_barrier(jnp.mean(pressure_now, axis=0, keepdims=True))
    mean_blocks = to_blocks(centre_field)
    dev_blocks = to_blocks(pressure_now - centre_field)
    packed = observe(mean_blocks, dev_blocks, observed_cell, observed_value, error_weight, observed_count)
    padded = jnp.pad(packed, ((1, 1), (1, 1), (0, 0), (0, 0)))
    local_obs, local_innov = select(padded, neighbour)
    analysed = lax.map(lambda parts: analyze(parts[0][None], parts[1][None], parts[2][None], parts[3][None])[0], (mean_blocks, dev_blocks, local_obs, local_innov))
    return (from_blocks(analysed), content_now)
```

```python
import math

import jax
import jax.numpy as jnp
from jax import lax
from jax.experimental import pallas as pl
from jax.experimental.pallas import tpu as pltpu
from jax.sharding import PartitionSpec as P

MEMBERS = 128
STEPS = 4
BR = 4
BC = 32
OBS_MAX = 16
NBR = 4
NS_ITERS = 7

PEERS = 16
SLABS = 8
OWN = 8
ROWS = 32
COLS = 4096
TILES = 32
PAD_ROWS = 48
BLOCKS = 64

inflation = 1.1
high = lax.Precision.HIGH
highest = lax.Precision.HIGHEST
root_weight = [
    math.exp(-0.25 * ((index // 3 - 1) ** 2 + (index % 3 - 1) ** 2)) for index in range(9)
]


def swap_groups(rows):
    group = lax.broadcasted_iota(jnp.int32, (8, 128), 1) // BC
    even = group % 2 == 0
    low = group < 2
    near = [None] * 4
    for i in (0, 2):
        near[i] = jnp.where(even, rows[i], pltpu.roll(rows[i + 1], BC, 1))
        near[i + 1] = jnp.where(even, pltpu.roll(rows[i], 128 - BC, 1), rows[i + 1])
    out = [None] * 4
    for i in (0, 1):
        out[i] = jnp.where(low, near[i], pltpu.roll(near[i + 2], 64, 1))
        out[i + 2] = jnp.where(low, pltpu.roll(near[i], 64, 1), near[i + 2])
    return out


def forecast_kernel(
    p_in, c_in, d_in, lp_in, lv_in, rate_in,
    c_out, gathered,
    p, p_other, c, c_other, lp, lv, rate, dif, dif_top, dif_low, keep, k_up, k_down, k_left, k_right,
    out_up, out_down, in_top, in_low, send,
    load_sem, p_sem, dif_send, dif_recv, halo_send, halo_recv, send_sem, recv_sem, own_sem, c_sem,
):
    mem = lax.axis_index("mem")
    slab = lax.axis_index("slab")
    above = lax.rem(slab + SLABS - 1, SLABS)
    below = lax.rem(slab + 1, SLABS)

    def load_p(tile):
        return pltpu.make_async_copy(
            p_in.at[:, :, pl.ds(pl.multiple_of(tile * 128, 128), 128)],
            p.at[tile + 1, :, pl.ds(8, ROWS), :],
            p_sem.at[tile],
        )

    loads = [
        pltpu.make_async_copy(src, dst, load_sem.at[i])
        for i, (src, dst) in enumerate(
            ((d_in, dif), (lp_in, lp), (lv_in, lv), (rate_in, rate), (c_in, c))
        )
    ]
    for load in loads[:1]:
        load.start()

    @pl.loop(0, TILES)
    def _(tile):
        load_p(tile).start()

    for load in loads[1:]:
        load.start()

    barrier = pltpu.get_barrier_semaphore()

    @pl.loop(1, PEERS)
    def _(i):
        pl.semaphore_signal(
            barrier, inc=1, device_id=(lax.rem(mem + i, PEERS), slab),
            device_id_type=pl.DeviceIdType.MESH,
        )

    for other in (above, below):
        pl.semaphore_signal(
            barrier, inc=1, device_id=(mem, other), device_id_type=pl.DeviceIdType.MESH
        )

    zero = jnp.zeros((8, 128), jnp.float32)
    for field in (p, p_other):
        for tile in (0, TILES + 1):
            for m in range(OWN):
                for i in range(PAD_ROWS // 8):
                    field[tile, m, i * 8 : i * 8 + 8, :] = zero

    pl.semaphore_wait(barrier, PEERS + 1)

    def dif_copy(i, src, dst, other):
        return pltpu.make_async_remote_copy(
            src_ref=src, dst_ref=dst, send_sem=dif_send.at[i], recv_sem=dif_recv.at[i],
            device_id=(mem, other), device_id_type=pl.DeviceIdType.MESH,
        )

    dif_copies = [
        dif_copy(0, d_in.at[pl.ds(24, 8)], dif_top, below),
        dif_copy(1, d_in.at[pl.ds(0, 8)], dif_low, above),
    ]
    for copy in dif_copies:
        copy.start()

    def halo_copy(step, i):
        src, dst, other = ((out_down, in_top, below), (out_up, in_low, above))[i]
        return pltpu.make_async_remote_copy(
            src_ref=src.at[step], dst_ref=dst.at[step],
            send_sem=halo_send.at[step, i], recv_sem=halo_recv.at[step, i],
            device_id=(mem, other), device_id_type=pl.DeviceIdType.MESH,
        )

    flat, flat_other = (
        field.reshape(TILES + 2, OWN * PAD_ROWS, 128) for field in (p, p_other)
    )

    def send_halo(step, source):

        @pl.loop(0, TILES)
        def _(tile):
            out_up[step, tile] = source[tile + 1, pl.ds(8, OWN, stride=PAD_ROWS), :]
            out_down[step, tile] = source[
                tile + 1, pl.ds(7 + ROWS, OWN, stride=PAD_ROWS), :
            ]

        for i in range(2):
            halo_copy(step, i).start()

    @pl.loop(0, TILES)
    def _(tile):
        load_p(tile).wait()

    send_halo(0, flat)

    for load in loads:
        load.wait()
    for copy in dif_copies:
        copy.wait()

    lane = lax.broadcasted_iota(jnp.int32, (8, 128), 1)
    line = lax.broadcasted_iota(jnp.int32, (8, 128), 0)
    first, last = lane == 0, lane == 127
    at_top, at_low = slab == 0, slab == SLABS - 1

    @pl.loop(0, TILES)
    def _(tile):
        here = pl.ds(pl.multiple_of(tile * 128, 128), 128)
        left = pl.ds(pl.multiple_of(jnp.maximum(tile - 1, 0) * 128, 128), 128)
        right = pl.ds(pl.multiple_of(jnp.minimum(tile + 1, TILES - 1) * 128, 128), 128)
        top_row = jnp.where(at_top, 0.0, dif_top[:, here])
        low_row = jnp.where(at_low, 0.0, dif_low[:, here])
        mids = [dif[i * 8 : i * 8 + 8, here] for i in range(4)]
        column = [top_row, *mids, low_row]
        for i in range(4):
            rows = slice(i * 8, i * 8 + 8)
            mid = mids[i]
            up = jnp.where(line == 0, pltpu.roll(column[i], 1, 0), pltpu.roll(mid, 1, 0))
            down = jnp.where(line == 7, pltpu.roll(column[i + 2], 7, 0), pltpu.roll(mid, 7, 0))
            next_left = jnp.where(tile == 0, 0.0, dif[rows, left])
            next_right = jnp.where(tile == TILES - 1, 0.0, dif[rows, right])
            west = jnp.where(first, pltpu.roll(next_left, 1, 1), pltpu.roll(mid, 1, 1))
            east = jnp.where(last, pltpu.roll(next_right, 127, 1), pltpu.roll(mid, 127, 1))
            sides = [0.1 * (mid + side) for side in (up, down, west, east)]
            for ref, side in zip((k_up, k_down, k_left, k_right), sides):
                ref[rows, here] = side
            keep[rows, here] = 1.0 - ((sides[0] + sides[1]) + (sides[2] + sides[3]))
            lv[rows, here] = lv[rows, here] * rate[rows, here]

    wide = 4

    def advance(now, content_now, later, content_later, row_tiles):

        @pl.loop(0, TILES // wide)
        def _(group):
            for row_tile in row_tiles:
                rows = slice(row_tile * 8, row_tile * 8 + 8)
                base = 8 + row_tile * 8
                heres = [
                    pl.ds(pl.multiple_of((group * wide + j) * 128, 128), 128) for j in range(wide)
                ]
                weights = [
                    [ref[rows, here] for ref in (keep, k_up, k_down, k_left, k_right, lp, lv, rate)]
                    for here in heres
                ]
                for m in range(OWN):
                    mids = [
                        now[group * wide + j, m, base : base + 8, :] for j in range(wide + 2)
                    ]
                    to_right = [pltpu.roll(mids[j], 1, 1) for j in range(wide + 1)]
                    to_left = [None] + [pltpu.roll(mids[j], 127, 1) for j in range(1, wide + 2)]
                    for j in range(wide):
                        keep_w, up_w, down_w, left_w, right_w, lp_w, lv_w, rate_w = weights[j]
                        tile = group * wide + j + 1
                        mid = mids[j + 1]
                        up = now[tile, m, base - 1 : base + 7, :]
                        down = now[tile, m, base + 1 : base + 9, :]
                        west = jnp.where(first, to_right[j], to_right[j + 1])
                        east = jnp.where(last, to_left[j + 2], to_left[j + 1])
                        content = content_now[m, rows, heres[j]]
                        inverse = pltpu.reciprocal(lp_w + jnp.abs(mid), approx=True)
                        release = rate_w * content - (lv_w * mid) * inverse
                        flow = (up_w * up + down_w * down) + (left_w * west + right_w * east)
                        later[tile, m, base : base + 8, :] = (
                            keep_w * mid + flow + release
                        )
                        content_later[m, rows, heres[j]] = content - release

    def one_step(step, now, content_now, later, content_later, flat_now, flat_later, more):
        advance(now, content_now, later, content_later, (1, 2))
        for i in range(2):
            halo_copy(step, i).wait()

        @pl.loop(0, TILES)
        def _(tile):
            top = jnp.where(at_top, 0.0, in_top[step, tile])
            low = jnp.where(at_low, 0.0, in_low[step, tile])
            flat_now[tile + 1, pl.ds(7, OWN, stride=PAD_ROWS), :] = top
            flat_now[tile + 1, pl.ds(8 + ROWS, OWN, stride=PAD_ROWS), :] = low

        advance(now, content_now, later, content_later, (0, 3))

        @pl.when(more)
        def _():
            send_halo(step + 1, flat_later)

    @pl.loop(0, STEPS // 2)
    def _(pair):
        one_step(2 * pair, p, c, p_other, c_other, flat, flat_other, True)
        one_step(2 * pair + 1, p_other, c_other, p, c, flat_other, flat, pair < STEPS // 2 - 1)

    store_c = pltpu.make_async_copy(c, c_out, c_sem)
    store_c.start()

    def to_blocks(target):
        for a in range(ROWS // BR):
            for j in range(2):
                lines = [
                    flat[target * 2 + j + 1, pl.ds(8 + a * BR + r, OWN, stride=PAD_ROWS), :]
                    for r in range(BR)
                ]
                blocks = swap_groups(lines)
                for b in range(4):
                    send[target, a * 8 + j * 4 + b] = blocks[b]

    mine = pl.ds(pl.multiple_of(mem * OWN, OWN), OWN)

    def block_copy(i):
        target = lax.rem(mem + i, PEERS)
        return pltpu.make_async_remote_copy(
            src_ref=send.at[target], dst_ref=gathered.at[:, mine, :],
            send_sem=send_sem.at[i], recv_sem=recv_sem.at[i],
            device_id=(target, slab), device_id_type=pl.DeviceIdType.MESH,
        )

    @pl.loop(1, PEERS)
    def _(i):
        to_blocks(lax.rem(mem + i, PEERS))
        block_copy(i).start()

    to_blocks(mem)
    own = pltpu.make_async_copy(send.at[mem], gathered.at[:, mine, :], own_sem)
    own.start()

    @pl.loop(1, PEERS)
    def _(i):
        block_copy(i).wait()

    own.wait()
    store_c.wait()


def forecast(pressure, content, diffusivity, langmuir_pressure, langmuir_volume, desorb_rate):
    field = (ROWS, COLS)
    f32 = jnp.float32
    anywhere = pl.BlockSpec(memory_space=pl.ANY)
    halo = pltpu.VMEM((STEPS, TILES, OWN, 128), f32)
    dma = pltpu.SemaphoreType.DMA
    return pl.pallas_call(
        forecast_kernel,
        out_shape=(
            jax.ShapeDtypeStruct(content.shape, f32),
            jax.ShapeDtypeStruct((BLOCKS, MEMBERS, BR * BC), f32),
        ),
        in_specs=[anywhere] * 6,
        out_specs=[anywhere] * 2,
        scratch_shapes=[
            *[pltpu.VMEM((TILES + 2, OWN, PAD_ROWS, 128), f32)] * 2,
            *[pltpu.VMEM((OWN, ROWS, COLS), f32)] * 2,
            *[pltpu.VMEM(field, f32)] * 4,
            *[pltpu.VMEM((8, COLS), f32)] * 2,
            *[pltpu.VMEM(field, f32)] * 5,
            *[halo] * 4,
            pltpu.VMEM((PEERS, BLOCKS, OWN, 128), f32),
            dma((5,)), dma((TILES,)), dma((2,)), dma((2,)),
            dma((STEPS, 2)), dma((STEPS, 2)), dma((PEERS,)), dma((PEERS,)), dma, dma,
        ],
        compiler_params=pltpu.CompilerParams(
            collective_id=0, has_side_effects=True, vmem_limit_bytes=58 << 20
        ),
        name="forecast",
    )(pressure, content, diffusivity, langmuir_pressure, langmuir_volume, desorb_rate)


def padded_2(cells, sides, width):
    for axis, dim in sides:
        count = lax.axis_size(axis)
        ends = count - 1
        head = lax.slice_in_dim(cells, 0, width, axis=dim)
        tail = lax.slice_in_dim(cells, cells.shape[dim] - width, cells.shape[dim], axis=dim)
        cells = jnp.concatenate(
            [
                lax.ppermute(tail, axis, [(i, (i + 1) % count) for i in range(ends)]),
                cells,
                lax.ppermute(head, axis, [((i + 1) % count, i) for i in range(ends)]),
            ],
            axis=dim,
        )
    return cells


def from_blocks(blocks):
    count_x, count_y, leading, cells = blocks.shape
    shaped = blocks.reshape(count_x, count_y, leading, BR, BC)
    return shaped.transpose(2, 0, 3, 1, 4).reshape(leading, count_x * BR, count_y * BC)


def observe(mean_blocks, dev_blocks, observed_cell, observed_value, error_weight, observed_count):
    onehot = (
        observed_cell[..., None] == jnp.arange(BR * BC, dtype=jnp.int32)[None, None, None, :]
    ).astype(jnp.float32)
    spread = jnp.einsum("abjc,abmc->abjm", onehot, dev_blocks, precision=highest)
    centre = jnp.einsum("abjc,abc->abj", onehot, mean_blocks[:, :, 0], precision=highest)
    live_mask = (
        jnp.arange(OBS_MAX, dtype=jnp.int32)[None, None, :] < observed_count[..., None]
    ).astype(jnp.float32)
    root_error = jnp.sqrt(error_weight) * live_mask
    scaled = spread * root_error[..., None]
    innovation = (observed_value - centre) * root_error
    row_pad = jnp.pad(innovation, ((0, 0), (0, 0), (0, MEMBERS - OBS_MAX)))
    return jnp.concatenate([scaled, row_pad[:, :, None, :]], axis=2)


def select(padded, neighbour):
    count_x, count_y = (neighbour.shape[0], neighbour.shape[1])
    chosen = jnp.zeros((count_x, count_y, NBR, OBS_MAX + 1, MEMBERS), jnp.float32)
    for offset_code in range(9):
        shift_x = offset_code // 3
        shift_y = offset_code % 3
        window = padded[shift_x : shift_x + count_x, shift_y : shift_y + count_y]
        weight = (neighbour == offset_code).astype(jnp.float32) * root_weight[offset_code]
        chosen = chosen + weight[..., None, None] * window[:, :, None]
    local_obs = chosen[:, :, :, :OBS_MAX, :].reshape(count_x, count_y, NBR * OBS_MAX, MEMBERS)
    local_innov = chosen[:, :, :, OBS_MAX, :OBS_MAX].reshape(count_x, count_y, NBR * OBS_MAX)
    return (local_obs, local_innov)


def analyze(mean_blocks, dev_blocks, local_obs, local_innov):
    gram_matrix = jnp.einsum("abom,abon->abmn", local_obs, local_obs, precision=high)
    pull_vector = jnp.einsum("abo,abom->abm", local_innov, local_obs, precision=highest)
    identity = jnp.eye(MEMBERS, dtype=jnp.float32)
    system = gram_matrix + (MEMBERS - 1) / inflation * identity
    trace_bound = jnp.trace(system, axis1=2, axis2=3)
    root_now = system / trace_bound[..., None, None]
    factor = 0.5 * (3.0 * identity - root_now)
    inverse_root = factor
    root_now = jnp.einsum("abij,abjk->abik", root_now, factor, precision=high)
    for sweep_index in range(1, NS_ITERS):
        product = jnp.einsum("abij,abjk->abik", inverse_root, root_now, precision=high)
        factor = 0.5 * (3.0 * identity - product)
        if sweep_index < NS_ITERS - 1:
            root_now = jnp.einsum("abij,abjk->abik", root_now, factor, precision=high)
        inverse_root = jnp.einsum("abij,abjk->abik", factor, inverse_root, precision=high)
    inverse_root = inverse_root / jnp.sqrt(trace_bound)[..., None, None]
    first_pass = jnp.einsum("abij,abj->abi", inverse_root, pull_vector, precision=highest)
    shift_mean = jnp.einsum("abij,abj->abi", inverse_root, first_pass, precision=highest)
    weights = math.sqrt(MEMBERS - 1) * inverse_root + shift_mean[..., :, None]
    return mean_blocks + jnp.einsum("abji,abjc->abic", weights, dev_blocks, precision=high)


def on_device(
    pressure, content, diffusivity, langmuir_pressure, langmuir_volume, desorb_rate,
    observed_cell, observed_value, error_weight, observed_count, neighbour,
):
    content_now, gathered = forecast(
        pressure, content, diffusivity, langmuir_pressure, langmuir_volume, desorb_rate
    )
    blocks = gathered.reshape(8, 8, MEMBERS, BR * BC)
    mean_blocks = jnp.mean(blocks, axis=2, keepdims=True)
    dev_blocks = blocks - mean_blocks
    packed = observe(
        mean_blocks, dev_blocks, observed_cell, observed_value, error_weight, observed_count
    )
    padded = padded_2(packed, (("mem", 1), ("slab", 0)), 1)
    local_obs, local_innov = select(padded, neighbour)
    analysed = analyze(mean_blocks, dev_blocks, local_obs, local_innov)
    return (from_blocks(analysed), content_now)


def solution(mesh):
    placed = (
        P("mem", "slab", None),
        P("mem", "slab", None),
        P("slab", None),
        P("slab", None),
        P("slab", None),
        P("slab", None),
        P("slab", "mem", None),
        P("slab", "mem", None),
        P("slab", "mem", None),
        P("slab", "mem"),
        P("slab", "mem", None),
    )
    return jax.shard_map(
        on_device,
        mesh=mesh,
        in_specs=placed,
        out_specs=(P(None, "slab", "mem"), P("mem", "slab", None)),
        check_vma=False,
    )
```

```python
import math

import jax
import jax.numpy as jnp
from jax import lax
from jax.experimental import pallas as pl
from jax.experimental.pallas import tpu as pltpu
from jax.sharding import PartitionSpec as P

MEMBERS = 128
STEPS = 4
BR = 4
BC = 32
OBS_MAX = 16
NBR = 4
NS_ITERS = 7

PEERS = 16
SLABS = 8
OWN = 8
ROWS = 32
COLS = 4096
TILES = 32
PAD_ROWS = 48
BLOCKS = 64
SIDE = 8
PAIRS = 8
HALF = NBR * OBS_MAX

inflation = 1.1
ridge = (MEMBERS - 1) / inflation
member_root = math.sqrt(MEMBERS - 1)
side_weight = math.exp(-0.25)
corner_weight = math.exp(-0.5)
mesh_ids = pl.DeviceIdType.MESH

ways = (
    (1, 0), (3, 0), (2, 2), (0, 2), (2, 0), (1, 1), (3, 3), (1, 3), (3, 1), (2, 1), (1, 2),
    (2, 3), (3, 2), (0, 1), (0, 3),
)
early = (0, 1)


def split(value):
    head = value.astype(jnp.bfloat16)
    return head, (value - head.astype(jnp.float32)).astype(jnp.bfloat16)


def product(left, head, tail):
    left_head, left_tail = split(left)
    both = jnp.concatenate([head, tail], axis=1)
    result = jnp.dot(
        jnp.concatenate([left_head, left_tail], axis=1),
        jnp.concatenate([both, both], axis=0),
        preferred_element_type=jnp.float32,
    )
    columns = head.shape[1]
    return result[:, :columns] + result[:, columns:]


def pair_product(left, right):
    same = (lax.broadcasted_iota(jnp.int32, (128, 128), 0) < HALF) == (
        lax.broadcasted_iota(jnp.int32, (128, 128), 1) < HALF
    )
    head, tail = (
        jnp.where(same, jnp.concatenate([part, part], axis=0), jnp.zeros((128, 128), jnp.bfloat16))
        for part in split(right)
    )
    return product(left, head, tail)


def swap_groups(rows):
    group = lax.broadcasted_iota(jnp.int32, (8, 128), 1) // BC
    even = group % 2 == 0
    low = group < 2
    near = [None] * 4
    for i in (0, 2):
        near[i] = jnp.where(even, rows[i], pltpu.roll(rows[i + 1], BC, 1))
        near[i + 1] = jnp.where(even, pltpu.roll(rows[i], 128 - BC, 1), rows[i + 1])
    out = [None] * 4
    for i in (0, 1):
        out[i] = jnp.where(low, near[i], pltpu.roll(near[i + 2], 64, 1))
        out[i + 2] = jnp.where(low, pltpu.roll(near[i], 64, 1), near[i + 2])
    return out


def forecast_kernel(
    p_in, c_in, d_in, lp_in, lv_in, rate_in, cells, values, roots, neighbour,
    c_out, gathered, weights_out,
    p, p_other, c, c_other, lp, lv, rate, dif, dif_top, dif_low, keep, k_up, k_down, k_left, k_right,
    out_up, out_down, in_top, in_low, send,
    all_cells, obs_send, obs_in, obs_pad, rows_z, innov_z, now_x, now_m, now_d, weights_now,
    load_sem, p_sem, dif_send, dif_recv, halo_send, halo_recv, send_sem, recv_sem, own_sem, c_sem,
    cell_send, cell_recv, obs_send_sem, obs_recv_sem, side_send, side_recv, weight_sem,
):
    mem = lax.axis_index("mem")
    slab = lax.axis_index("slab")
    above = lax.rem(slab + SLABS - 1, SLABS)
    below = lax.rem(slab + 1, SLABS)

    def load_p(tile):
        return pltpu.make_async_copy(
            p_in.at[:, :, pl.ds(pl.multiple_of(tile * 128, 128), 128)],
            p.at[tile + 1, :, pl.ds(8, ROWS), :],
            p_sem.at[tile],
        )

    loads = [
        pltpu.make_async_copy(src, dst, load_sem.at[i])
        for i, (src, dst) in enumerate(
            ((d_in, dif), (lp_in, lp), (lv_in, lv), (rate_in, rate), (c_in, c))
        )
    ]
    for load in loads[:1]:
        load.start()

    @pl.loop(0, TILES)
    def _(tile):
        load_p(tile).start()

    for load in loads[1:]:
        load.start()

    barrier = pltpu.get_barrier_semaphore()

    @pl.loop(1, PEERS)
    def _(i):
        pl.semaphore_signal(
            barrier, inc=1, device_id=(lax.rem(mem + i, PEERS), slab),
            device_id_type=pl.DeviceIdType.MESH,
        )

    for other in (above, below):
        pl.semaphore_signal(
            barrier, inc=1, device_id=(mem, other), device_id_type=pl.DeviceIdType.MESH
        )

    zero = jnp.zeros((8, 128), jnp.float32)
    for field in (p, p_other):
        for tile in (0, TILES + 1):
            for m in range(OWN):
                for i in range(PAD_ROWS // 8):
                    field[tile, m, i * 8 : i * 8 + 8, :] = zero

    pl.semaphore_wait(barrier, PEERS + 1)

    def dif_copy(i, src, dst, other):
        return pltpu.make_async_remote_copy(
            src_ref=src, dst_ref=dst, send_sem=dif_send.at[i], recv_sem=dif_recv.at[i],
            device_id=(mem, other), device_id_type=pl.DeviceIdType.MESH,
        )

    def cell_copy(i):
        return pltpu.make_async_remote_copy(
            src_ref=cells, dst_ref=all_cells.at[mem],
            send_sem=cell_send.at[i], recv_sem=cell_recv.at[i],
            device_id=(lax.rem(mem + i, PEERS), slab), device_id_type=mesh_ids,
        )

    @pl.loop(1, PEERS)
    def _(i):
        cell_copy(i).start()

    all_cells[mem] = cells[...]

    dif_copies = [
        dif_copy(0, d_in.at[pl.ds(24, 8)], dif_top, below),
        dif_copy(1, d_in.at[pl.ds(0, 8)], dif_low, above),
    ]
    for copy in dif_copies:
        copy.start()

    def halo_copy(step, i):
        src, dst, other = ((out_down, in_top, below), (out_up, in_low, above))[i]
        return pltpu.make_async_remote_copy(
            src_ref=src.at[step], dst_ref=dst.at[step],
            send_sem=halo_send.at[step, i], recv_sem=halo_recv.at[step, i],
            device_id=(mem, other), device_id_type=pl.DeviceIdType.MESH,
        )

    flat, flat_other = (
        field.reshape(TILES + 2, OWN * PAD_ROWS, 128) for field in (p, p_other)
    )

    def send_halo(step, source):

        @pl.loop(0, TILES)
        def _(tile):
            out_up[step, tile] = source[tile + 1, pl.ds(8, OWN, stride=PAD_ROWS), :]
            out_down[step, tile] = source[
                tile + 1, pl.ds(7 + ROWS, OWN, stride=PAD_ROWS), :
            ]

        for i in range(2):
            halo_copy(step, i).start()

    @pl.loop(0, TILES)
    def _(tile):
        load_p(tile).wait()

    send_halo(0, flat)

    for load in loads:
        load.wait()
    for copy in dif_copies:
        copy.wait()

    lane = lax.broadcasted_iota(jnp.int32, (8, 128), 1)
    line = lax.broadcasted_iota(jnp.int32, (8, 128), 0)
    first, last = lane == 0, lane == 127
    at_top, at_low = slab == 0, slab == SLABS - 1

    @pl.loop(0, TILES)
    def _(tile):
        here = pl.ds(pl.multiple_of(tile * 128, 128), 128)
        left = pl.ds(pl.multiple_of(jnp.maximum(tile - 1, 0) * 128, 128), 128)
        right = pl.ds(pl.multiple_of(jnp.minimum(tile + 1, TILES - 1) * 128, 128), 128)
        top_row = jnp.where(at_top, 0.0, dif_top[:, here])
        low_row = jnp.where(at_low, 0.0, dif_low[:, here])
        mids = [dif[i * 8 : i * 8 + 8, here] for i in range(4)]
        column = [top_row, *mids, low_row]
        for i in range(4):
            rows = slice(i * 8, i * 8 + 8)
            mid = mids[i]
            up = jnp.where(line == 0, pltpu.roll(column[i], 1, 0), pltpu.roll(mid, 1, 0))
            down = jnp.where(line == 7, pltpu.roll(column[i + 2], 7, 0), pltpu.roll(mid, 7, 0))
            next_left = jnp.where(tile == 0, 0.0, dif[rows, left])
            next_right = jnp.where(tile == TILES - 1, 0.0, dif[rows, right])
            west = jnp.where(first, pltpu.roll(next_left, 1, 1), pltpu.roll(mid, 1, 1))
            east = jnp.where(last, pltpu.roll(next_right, 127, 1), pltpu.roll(mid, 127, 1))
            sides = [0.1 * (mid + side) for side in (up, down, west, east)]
            for ref, side in zip((k_up, k_down, k_left, k_right), sides):
                ref[rows, here] = side
            keep[rows, here] = 1.0 - ((sides[0] + sides[1]) + (sides[2] + sides[3]))
            lv[rows, here] = lv[rows, here] * rate[rows, here]

    wide = 4

    def advance(now, content_now, later, content_later, row_tiles):

        @pl.loop(0, TILES // wide)
        def _(group):
            for row_tile in row_tiles:
                rows = slice(row_tile * 8, row_tile * 8 + 8)
                base = 8 + row_tile * 8
                heres = [
                    pl.ds(pl.multiple_of((group * wide + j) * 128, 128), 128) for j in range(wide)
                ]
                weights = [
                    [ref[rows, here] for ref in (keep, k_up, k_down, k_left, k_right, lp, lv, rate)]
                    for here in heres
                ]
                for m in range(OWN):
                    mids = [
                        now[group * wide + j, m, base : base + 8, :] for j in range(wide + 2)
                    ]
                    to_right = [pltpu.roll(mids[j], 1, 1) for j in range(wide + 1)]
                    to_left = [None] + [pltpu.roll(mids[j], 127, 1) for j in range(1, wide + 2)]
                    for j in range(wide):
                        keep_w, up_w, down_w, left_w, right_w, lp_w, lv_w, rate_w = weights[j]
                        tile = group * wide + j + 1
                        mid = mids[j + 1]
                        up = now[tile, m, base - 1 : base + 7, :]
                        down = now[tile, m, base + 1 : base + 9, :]
                        west = jnp.where(first, to_right[j], to_right[j + 1])
                        east = jnp.where(last, to_left[j + 2], to_left[j + 1])
                        content = content_now[m, rows, heres[j]]
                        inverse = pltpu.reciprocal(lp_w + jnp.abs(mid), approx=True)
                        release = rate_w * content - (lv_w * mid) * inverse
                        flow = (up_w * up + down_w * down) + (left_w * west + right_w * east)
                        later[tile, m, base : base + 8, :] = (
                            keep_w * mid + flow + release
                        )
                        content_later[m, rows, heres[j]] = content - release

    def one_step(step, now, content_now, later, content_later, flat_now, flat_later, more):
        advance(now, content_now, later, content_later, (1, 2))
        for i in range(2):
            halo_copy(step, i).wait()

        @pl.loop(0, TILES)
        def _(tile):
            top = jnp.where(at_top, 0.0, in_top[step, tile])
            low = jnp.where(at_low, 0.0, in_low[step, tile])
            flat_now[tile + 1, pl.ds(7, OWN, stride=PAD_ROWS), :] = top
            flat_now[tile + 1, pl.ds(8 + ROWS, OWN, stride=PAD_ROWS), :] = low

        advance(now, content_now, later, content_later, (0, 3))

        @pl.when(more)
        def _():
            send_halo(step + 1, flat_later)

    @pl.loop(0, STEPS // 2)
    def _(pair):
        one_step(2 * pair, p, c, p_other, c_other, flat, flat_other, True)
        one_step(2 * pair + 1, p_other, c_other, p, c, flat_other, flat, pair < STEPS // 2 - 1)

    store_c = pltpu.make_async_copy(c, c_out, c_sem)
    store_c.start()

    @pl.loop(1, PEERS)
    def _(i):
        cell_copy(i).wait()

    slot_group = lane // OBS_MAX

    def to_blocks(target):
        for a in range(SIDE):
            index = jnp.broadcast_to(all_cells[target, a : a + 1, :], (OWN, 128))
            observed = jnp.zeros((OWN, 128), jnp.float32)
            for j in range(2):
                lines = [
                    flat[target * 2 + j + 1, pl.ds(8 + a * BR + r, OWN, stride=PAD_ROWS), :]
                    for r in range(BR)
                ]
                blocks = swap_groups(lines)
                for b in range(4):
                    send[target, a * SIDE + j * 4 + b] = blocks[b]
                    picked = jnp.take_along_axis(blocks[b], index, axis=1)
                    observed = jnp.where(slot_group == j * 4 + b, picked, observed)
            obs_send[target, a] = observed

    mine = pl.ds(pl.multiple_of(mem * OWN, OWN), OWN)

    def obs_copy(i):
        target = lax.rem(mem + i, PEERS)
        return pltpu.make_async_remote_copy(
            src_ref=obs_send.at[target], dst_ref=obs_in.at[:, mine, :],
            send_sem=obs_send_sem.at[i], recv_sem=obs_recv_sem.at[i],
            device_id=(target, slab), device_id_type=mesh_ids,
        )

    def block_copy(i, way):
        target = lax.rem(mem // 4 + way[0], 4) * 4 + lax.rem(mem + way[1], 4)
        return pltpu.make_async_remote_copy(
            src_ref=send.at[target], dst_ref=gathered.at[:, mine, :],
            send_sem=send_sem.at[i], recv_sem=recv_sem.at[i],
            device_id=(target, slab), device_id_type=mesh_ids,
        )

    @pl.loop(1, PEERS)
    def _(i):
        to_blocks(lax.rem(mem + i, PEERS))
        obs_copy(i).start()

    to_blocks(mem)
    for i in early:
        block_copy(i, ways[i]).start()
    own = pltpu.make_async_copy(send.at[mem], gathered.at[:, mine, :], own_sem.at[0])
    own.start()
    own_obs = pltpu.make_async_copy(obs_send.at[mem], obs_in.at[:, mine, :], own_sem.at[1])
    own_obs.start()
    own_obs.wait()

    @pl.loop(1, PEERS)
    def _(i):
        obs_copy(i).wait()

    @pl.loop(0, SIDE)
    def _(a):
        seen = obs_in[a]
        centre = jnp.mean(seen, axis=0, keepdims=True)
        root = roots[pl.ds(a, 1), :]
        spread = ((seen - centre) * root).T
        innovation = jnp.broadcast_to((values[pl.ds(a, 1), :] - centre) * root, (128, 128)).T
        for b in range(SIDE):
            obs_pad[a + 1, b + 1, 0:OBS_MAX, :] = spread[b * OBS_MAX : (b + 1) * OBS_MAX]
            obs_pad[a + 1, b + 1, OBS_MAX:, :] = innovation[b * OBS_MAX : (b + 1) * OBS_MAX]

    def side_copy(i):
        src, dst, device = (
            (obs_pad.at[1:9, 8], obs_pad.at[1:9, 0], (lax.rem(mem + 1, PEERS), slab)),
            (obs_pad.at[1:9, 1], obs_pad.at[1:9, 9], (lax.rem(mem + PEERS - 1, PEERS), slab)),
            (obs_pad.at[8], obs_pad.at[0], (mem, below)),
            (obs_pad.at[1], obs_pad.at[9], (mem, above)),
        )[i]
        return pltpu.make_async_remote_copy(
            src_ref=src, dst_ref=dst, send_sem=side_send.at[i], recv_sem=side_recv.at[i],
            device_id=device, device_id_type=mesh_ids,
        )

    blank = jnp.zeros((2 * OBS_MAX, 128), jnp.float32)
    for sides, conditions in (
        ((0, 1), (mem == 0, mem == PEERS - 1)),
        ((2, 3), (at_top, at_low)),
    ):
        for i in sides:
            side_copy(i).start()
        for i in sides:
            side_copy(i).wait()
        if sides[0] == 0:
            for i in range(len(early), len(ways)):
                block_copy(i, ways[i]).start()
        for i, condition in zip(sides, conditions):

            @pl.when(condition)
            def _(i=i):
                @pl.loop(*((1, SIDE + 1) if i < 2 else (0, SIDE + 2)))
                def _(place):
                    if i < 2:
                        obs_pad[place, 0 if i == 0 else SIDE + 1] = blank
                    else:
                        obs_pad[0 if i == 2 else SIDE + 1, place] = blank

    def weight_copy(group):
        part = pl.ds(group * 2 * PAIRS, 2 * PAIRS)
        return pltpu.make_async_copy(
            weights_now.at[part], weights_out.at[part], weight_sem.at[group]
        )

    half_lane = lax.broadcasted_iota(jnp.int32, (1, 128), 1) < HALF
    diagonal = lax.broadcasted_iota(jnp.int32, (HALF, 128), 0) == lax.rem(
        lax.broadcasted_iota(jnp.int32, (HALF, 128), 1), HALF
    )
    pair_eye = jnp.where(diagonal, 1.0, 0.0)
    eye = lax.broadcasted_iota(jnp.int32, (128, 128), 0) == lax.broadcasted_iota(
        jnp.int32, (128, 128), 1
    )
    no_rows = jnp.zeros((HALF, 128), jnp.float32)

    @pl.loop(0, BLOCKS // (2 * PAIRS))
    def _(group):
        start = []
        for pair in range(PAIRS):
            for i in range(2 * NBR):
                place = 2 * pair + i // NBR
                a = group * (PAIRS // 4) + place // SIDE
                b = place % SIDE
                code = neighbour[a, b * NBR + i % NBR]
                down_by = lax.div(code, 3)
                right_by = code - 3 * down_by
                block = obs_pad[a + down_by, b + right_by]
                far = (down_by != 1).astype(jnp.int32) + (right_by != 1).astype(jnp.int32)
                weight = jnp.where(
                    far == 0, 1.0, jnp.where(far == 1, side_weight, corner_weight)
                )
                rows_z[pair, i * OBS_MAX : (i + 1) * OBS_MAX, :] = weight * block[:OBS_MAX]
                innov_z[pair, i * OBS_MAX : (i + 1) * OBS_MAX, :] = weight * block[OBS_MAX:]
        rows = [rows_z[pair] for pair in range(PAIRS)]
        grams = [product(z, *split(z.T)) for z in rows]
        smalls = [jnp.where(half_lane, gram[:HALF], gram[HALF:]) for gram in grams]
        traces = [
            jnp.sum(jnp.where(diagonal, small, 0.0), axis=0, keepdims=True) for small in smalls
        ]
        totals = [
            [
                MEMBERS * ridge + jnp.sum(jnp.where(side, trace, 0.0), axis=1, keepdims=True)
                for side in (half_lane, jnp.logical_not(half_lane))
            ]
            for trace in traces
        ]
        for pair, (small, total) in enumerate(zip(smalls, totals)):
            scale = 1.0 / jnp.where(half_lane, total[0], total[1])
            low = ridge * scale
            now_x[pair] = small * scale + low * pair_eye
            now_m[pair] = no_rows
            now_d[pair] = pair_eye
            start.append((low, jnp.ones_like(low)))

        def sweep(_, carry):
            states = [(now_x[i], now_m[i], now_d[i]) for i in range(PAIRS)]
            by_x = [
                pair_product(jnp.concatenate(state, axis=0), state[0]) for state in states
            ]
            factors = [
                0.25 * result[:HALF] - 1.5 * state[0] + 2.25 * pair_eye
                for result, state in zip(by_x, states)
            ]
            by_f = [
                pair_product(jnp.concatenate([x, d], axis=0), factor)
                for (x, _, d), factor in zip(states, factors)
            ]
            ahead = []
            later = []
            for (x, m, d), (low, gain), first, second in zip(states, carry, by_x, by_f):
                new_d = (
                    second[HALF:]
                    + (0.25 * low) * first[2 * HALF :]
                    + (0.25 * low * (low - 6.0)) * d
                )
                new_m = 1.5 * m - 0.5 * first[HALF : 2 * HALF] - (0.5 * gain) * d
                later.append((second[:HALF], new_m, new_d))
                shrink = 1.5 - 0.5 * low
                ahead.append((low * shrink * shrink, gain * shrink))
            for i in range(PAIRS):
                now_x[i], now_m[i], now_d[i] = later[i]
            return tuple(ahead)

        last_low = lax.fori_loop(0, NS_ITERS - 1, sweep, tuple(start))
        states = [(now_x[i], now_m[i], now_d[i]) for i in range(PAIRS)]
        rows = [rows_z[pair] for pair in range(PAIRS)]
        by_x = [pair_product(m, x) for x, m, _ in states]
        ends = []
        for (_, m, d), (_, gain), total, result in zip(states, last_low, totals, by_x):
            both = jnp.where(half_lane, total[0], total[1])
            m = 1.5 * m - 0.5 * result - (0.5 * gain) * d
            m = m * (1.0 / (both * jnp.sqrt(both)))
            ends.append(
                jnp.concatenate(
                    [jnp.where(half_lane, m, 0.0), jnp.where(half_lane, 0.0, m)], axis=0
                )
            )
        by_z = [product(end, *split(z)) for end, z in zip(ends, rows)]
        wide_z = [
            jnp.concatenate(
                [
                    jnp.concatenate([m_z[:HALF], no_rows], axis=0),
                    jnp.concatenate([no_rows, m_z[HALF:]], axis=0),
                ],
                axis=1,
            )
            for m_z in by_z
        ]
        roots_both = [product(z.T, *split(right)) for z, right in zip(rows, wide_z)]
        gains = []
        pulls = []
        for pair, (z, total) in enumerate(zip(rows, totals)):
            for side in range(2):
                low = ridge / total[side]
                gain = 1.0 / jnp.sqrt(total[side])
                for _ in range(NS_ITERS):
                    shrink = 1.5 - 0.5 * low
                    low, gain = low * shrink * shrink, gain * shrink
                gains.append(gain)
                own_rows = slice(side * HALF, side * HALF + HALF)
                pulls.append(
                    jnp.sum(innov_z[pair, own_rows] * z[own_rows], axis=0, keepdims=True)
                )
        for i, (gain, pull) in enumerate(zip(gains, pulls)):
            column = i % 2 * 128
            root = roots_both[i // 2][:, column : column + 128] + jnp.where(eye, gain, 0.0)
            first_pass = jnp.sum(root * pull, axis=1, keepdims=True)
            shift = jnp.sum(root * first_pass, axis=0, keepdims=True)
            weights_now[group * 2 * PAIRS + i] = member_root * root + shift
        weight_copy(group).start()

    @pl.loop(0, BLOCKS // (2 * PAIRS))
    def _(group):
        weight_copy(group).wait()

    for i, way in enumerate(ways):
        block_copy(i, way).wait()
    own.wait()
    store_c.wait()


def forecast(fields, cells, values, roots, neighbour):
    field = (ROWS, COLS)
    f32 = jnp.float32
    anywhere = pl.BlockSpec(memory_space=pl.ANY)
    local = pl.BlockSpec(memory_space=pltpu.VMEM)
    halo = pltpu.VMEM((STEPS, TILES, OWN, 128), f32)
    dma = pltpu.SemaphoreType.DMA
    square = (BLOCKS, MEMBERS, 128)
    return pl.pallas_call(
        forecast_kernel,
        out_shape=(
            jax.ShapeDtypeStruct((OWN, ROWS, COLS), f32),
            jax.ShapeDtypeStruct(square, f32),
            jax.ShapeDtypeStruct(square, f32),
        ),
        in_specs=[anywhere] * 6 + [local] * 3 + [pl.BlockSpec(memory_space=pltpu.SMEM)],
        out_specs=[anywhere] * 3,
        scratch_shapes=[
            *[pltpu.VMEM((TILES + 2, OWN, PAD_ROWS, 128), f32)] * 2,
            *[pltpu.VMEM((OWN, ROWS, COLS), f32)] * 2,
            *[pltpu.VMEM(field, f32)] * 4,
            *[pltpu.VMEM((8, COLS), f32)] * 2,
            *[pltpu.VMEM(field, f32)] * 5,
            *[halo] * 4,
            pltpu.VMEM((PEERS, BLOCKS, OWN, 128), f32),
            pltpu.VMEM((PEERS, SIDE, 128), jnp.int32),
            pltpu.VMEM((PEERS, SIDE, OWN, 128), f32),
            pltpu.VMEM((SIDE, MEMBERS, 128), f32),
            pltpu.VMEM((SIDE + 2, SIDE + 2, 2 * OBS_MAX, 128), f32),
            *[pltpu.VMEM((PAIRS, 2 * HALF, 128), f32)] * 2,
            *[pltpu.VMEM((PAIRS, HALF, 128), f32)] * 3,
            pltpu.VMEM((BLOCKS, MEMBERS, 128), f32),
            dma((5,)), dma((TILES,)), dma((2,)), dma((2,)),
            dma((STEPS, 2)), dma((STEPS, 2)), dma((PEERS,)), dma((PEERS,)), dma((2,)), dma,
            dma((PEERS,)), dma((PEERS,)), dma((PEERS,)), dma((PEERS,)), dma((4,)), dma((4,)),
            dma((SIDE,)),
        ],
        compiler_params=pltpu.CompilerParams(
            collective_id=0, has_side_effects=True, vmem_limit_bytes=60 << 20
        ),
        name="forecast",
    )(*fields, cells, values, roots, neighbour)


def update_kernel(gathered, weights, content, analysis, content_out, lines):
    flat = lines.reshape(2, MEMBERS * 8, 128)

    @pl.loop(0, 4)
    def _(part):
        a, j = part // 2, lax.rem(part, 2)
        updated = []
        for b in range(4):
            place = a * SIDE + j * 4 + b
            field = gathered[place]
            centre = jnp.mean(field, axis=0, keepdims=True)
            head, tail = split(field - centre)
            updated.append(product(weights[place], head, tail) + centre)
        for group in range(MEMBERS // 8):
            rows = swap_groups([block[group * 8 : group * 8 + 8] for block in updated])
            for r in range(BR):
                flat[j, pl.ds(group * 64 + a * BR + r, 8, stride=8), :] = rows[r]

    for j in range(2):
        analysis[:, :, j * 128 : j * 128 + 128] = lines[j]
    content_out[...] = content[...]


def update(gathered, weights, content):
    f32 = jnp.float32
    square = pl.BlockSpec((2 * SIDE, MEMBERS, 128), lambda i: (i, 0, 0))
    own = pl.BlockSpec((OWN, 8, COLS), lambda i: (0, i, 0))
    return pl.pallas_call(
        update_kernel,
        grid=(4,),
        out_shape=(
            jax.ShapeDtypeStruct((MEMBERS, ROWS, 2 * 128), f32),
            jax.ShapeDtypeStruct(content.shape, f32),
        ),
        in_specs=[square, square, own],
        out_specs=[pl.BlockSpec((MEMBERS, 8, 2 * 128), lambda i: (0, i, 0)), own],
        scratch_shapes=[pltpu.VMEM((2, MEMBERS, 8, 128), f32)],
        compiler_params=pltpu.CompilerParams(vmem_limit_bytes=40 << 20),
        name="update",
    )(gathered, weights, content)


def on_device(
    pressure, content, diffusivity, langmuir_pressure, langmuir_volume, desorb_rate,
    observed_cell, observed_value, error_weight, observed_count, neighbour,
):
    live = jnp.arange(OBS_MAX, dtype=jnp.int32) < observed_count[..., None]
    root_error = jnp.sqrt(error_weight) * live.astype(jnp.float32)
    content_now, gathered, weights = forecast(
        (pressure, content, diffusivity, langmuir_pressure, langmuir_volume, desorb_rate),
        observed_cell.reshape(SIDE, 128),
        observed_value.reshape(SIDE, 128),
        root_error.reshape(SIDE, 128),
        neighbour.reshape(SIDE, SIDE * NBR),
    )
    return update(gathered, weights, content_now)


def solution(mesh):
    placed = (
        P("mem", "slab", None),
        P("mem", "slab", None),
        P("slab", None),
        P("slab", None),
        P("slab", None),
        P("slab", None),
        P("slab", "mem", None),
        P("slab", "mem", None),
        P("slab", "mem", None),
        P("slab", "mem"),
        P("slab", "mem", None),
    )
    return jax.shard_map(
        on_device,
        mesh=mesh,
        in_specs=placed,
        out_specs=(P(None, "slab", "mem"), P("mem", "slab", None)),
        check_vma=False,
    )
```

```python
import math

import jax
import jax.numpy as jnp
from jax import lax
from jax.experimental import pallas as pl
from jax.experimental.pallas import tpu as pltpu
from jax.sharding import PartitionSpec as P

MEMBERS = 128
STEPS = 4
BR = 4
BC = 32
OBS_MAX = 16
NBR = 4
NS_ITERS = 7

PEERS = 16
SLABS = 8
OWN = 8
ROWS = 32
COLS = 4096
TILES = 32
PAD_ROWS = 48
BLOCKS = 64
SIDE = 8
PAIRS = 8
PARTS = 4
HALF = NBR * OBS_MAX

inflation = 1.1
ridge = (MEMBERS - 1) / inflation
member_root = math.sqrt(MEMBERS - 1)
side_weight = math.exp(-0.25)
corner_weight = math.exp(-0.5)
mesh_ids = pl.DeviceIdType.MESH

ways = (
    (1, 0), (3, 0), (2, 2), (0, 2), (2, 0), (1, 1), (3, 3), (1, 3), (3, 1), (2, 1), (1, 2),
    (2, 3), (3, 2), (0, 1), (0, 3),
)


def split(value):
    head = value.astype(jnp.bfloat16)
    return head, (value - head.astype(jnp.float32)).astype(jnp.bfloat16)


def product(left, head, tail):
    left_head, left_tail = split(left)
    both = jnp.concatenate([head, tail], axis=1)
    result = jnp.dot(
        jnp.concatenate([left_head, left_tail], axis=1),
        jnp.concatenate([both, both], axis=0),
        preferred_element_type=jnp.float32,
    )
    columns = head.shape[1]
    return result[:, :columns] + result[:, columns:]


def pair_product(left, right):
    same = (lax.broadcasted_iota(jnp.int32, (128, 128), 0) < HALF) == (
        lax.broadcasted_iota(jnp.int32, (128, 128), 1) < HALF
    )
    head, tail = (
        jnp.where(same, jnp.concatenate([part, part], axis=0), jnp.zeros((128, 128), jnp.bfloat16))
        for part in split(right)
    )
    return product(left, head, tail)


def swap_groups(rows):
    group = lax.broadcasted_iota(jnp.int32, (8, 128), 1) // BC
    even = group % 2 == 0
    low = group < 2
    near = [None] * 4
    for i in (0, 2):
        near[i] = jnp.where(even, rows[i], pltpu.roll(rows[i + 1], BC, 1))
        near[i + 1] = jnp.where(even, pltpu.roll(rows[i], 128 - BC, 1), rows[i + 1])
    out = [None] * 4
    for i in (0, 1):
        out[i] = jnp.where(low, near[i], pltpu.roll(near[i + 2], 64, 1))
        out[i + 2] = jnp.where(low, pltpu.roll(near[i], 64, 1), near[i + 2])
    return out


def assimilate_kernel(
    p_in, c_in, d_in, lp_in, lv_in, rate_in, cell_in, value_in, error_in, count_in, neighbour,
    analysis, c_out,
    p, p_other, c, c_other, lp, lv, rate, dif, dif_top, dif_low, keep, k_up, k_down, k_left, k_right,
    out_up, out_down, in_top, in_low, send,
    cells, values, roots, all_cells, obs_send, obs_in, obs_pad,
    rows_z, innov_z, now_x, now_m, now_d, weights_now, gathered, lines,
    load_sem, p_sem, dif_send, dif_recv, halo_send, halo_recv, send_sem, recv_sem, own_sem, c_sem,
    cell_send, cell_recv, obs_send_sem, obs_recv_sem, side_send, side_recv, out_sem,
):
    mem = lax.axis_index("mem")
    slab = lax.axis_index("slab")
    above = lax.rem(slab + SLABS - 1, SLABS)
    below = lax.rem(slab + 1, SLABS)

    def load_p(tile):
        return pltpu.make_async_copy(
            p_in.at[:, :, pl.ds(pl.multiple_of(tile * 128, 128), 128)],
            p.at[tile + 1, :, pl.ds(8, ROWS), :],
            p_sem.at[tile],
        )

    loads = [
        pltpu.make_async_copy(src, dst, load_sem.at[i])
        for i, (src, dst) in enumerate(
            ((d_in, dif), (lp_in, lp), (lv_in, lv), (rate_in, rate), (c_in, c))
        )
    ]
    for load in loads[:1]:
        load.start()

    @pl.loop(0, TILES)
    def _(tile):
        load_p(tile).start()

    for load in loads[1:]:
        load.start()

    lane = lax.broadcasted_iota(jnp.int32, (8, 128), 1)
    line = lax.broadcasted_iota(jnp.int32, (8, 128), 0)
    slot_group = lane // OBS_MAX

    def lay_out(piece_of):
        out = piece_of(0)
        for b in range(1, SIDE):
            out = jnp.where(slot_group == b, piece_of(b), out)
        return out

    def slots_of(ref):
        return lay_out(lambda b: jnp.concatenate([ref[:, b, :]] * SIDE, axis=1))

    cells[...] = slots_of(cell_in)
    values[...] = slots_of(value_in)
    counts = lay_out(lambda b: jnp.broadcast_to(count_in[:, b : b + 1], (SIDE, 128)))
    live = lax.rem(lane, OBS_MAX) < counts
    roots[...] = jnp.where(live, jnp.sqrt(slots_of(error_in)), 0.0)

    barrier = pltpu.get_barrier_semaphore()

    @pl.loop(1, PEERS)
    def _(i):
        pl.semaphore_signal(
            barrier, inc=1, device_id=(lax.rem(mem + i, PEERS), slab),
            device_id_type=pl.DeviceIdType.MESH,
        )

    for other in (above, below):
        pl.semaphore_signal(
            barrier, inc=1, device_id=(mem, other), device_id_type=pl.DeviceIdType.MESH
        )

    zero = jnp.zeros((8, 128), jnp.float32)
    for field in (p, p_other):
        for tile in (0, TILES + 1):
            for m in range(OWN):
                for i in range(PAD_ROWS // 8):
                    field[tile, m, i * 8 : i * 8 + 8, :] = zero

    pl.semaphore_wait(barrier, PEERS + 1)

    def dif_copy(i, src, dst, other):
        return pltpu.make_async_remote_copy(
            src_ref=src, dst_ref=dst, send_sem=dif_send.at[i], recv_sem=dif_recv.at[i],
            device_id=(mem, other), device_id_type=pl.DeviceIdType.MESH,
        )

    def cell_copy(i):
        return pltpu.make_async_remote_copy(
            src_ref=cells, dst_ref=all_cells.at[mem],
            send_sem=cell_send.at[i], recv_sem=cell_recv.at[i],
            device_id=(lax.rem(mem + i, PEERS), slab), device_id_type=mesh_ids,
        )

    @pl.loop(1, PEERS)
    def _(i):
        cell_copy(i).start()

    all_cells[mem] = cells[...]

    dif_copies = [
        dif_copy(0, d_in.at[pl.ds(24, 8)], dif_top, below),
        dif_copy(1, d_in.at[pl.ds(0, 8)], dif_low, above),
    ]
    for copy in dif_copies:
        copy.start()

    def halo_copy(step, i):
        src, dst, other = ((out_down, in_top, below), (out_up, in_low, above))[i]
        return pltpu.make_async_remote_copy(
            src_ref=src.at[step], dst_ref=dst.at[step],
            send_sem=halo_send.at[step, i], recv_sem=halo_recv.at[step, i],
            device_id=(mem, other), device_id_type=pl.DeviceIdType.MESH,
        )

    flat, flat_other = (
        field.reshape(TILES + 2, OWN * PAD_ROWS, 128) for field in (p, p_other)
    )

    def send_halo(step, source):

        @pl.loop(0, TILES)
        def _(tile):
            out_up[step, tile] = source[tile + 1, pl.ds(8, OWN, stride=PAD_ROWS), :]
            out_down[step, tile] = source[
                tile + 1, pl.ds(7 + ROWS, OWN, stride=PAD_ROWS), :
            ]

        for i in range(2):
            halo_copy(step, i).start()

    @pl.loop(0, TILES)
    def _(tile):
        load_p(tile).wait()

    send_halo(0, flat)

    for load in loads:
        load.wait()
    for copy in dif_copies:
        copy.wait()

    first, last = lane == 0, lane == 127
    at_top, at_low = slab == 0, slab == SLABS - 1

    @pl.loop(0, TILES)
    def _(tile):
        here = pl.ds(pl.multiple_of(tile * 128, 128), 128)
        left = pl.ds(pl.multiple_of(jnp.maximum(tile - 1, 0) * 128, 128), 128)
        right = pl.ds(pl.multiple_of(jnp.minimum(tile + 1, TILES - 1) * 128, 128), 128)
        top_row = jnp.where(at_top, 0.0, dif_top[:, here])
        low_row = jnp.where(at_low, 0.0, dif_low[:, here])
        mids = [dif[i * 8 : i * 8 + 8, here] for i in range(4)]
        column = [top_row, *mids, low_row]
        for i in range(4):
            rows = slice(i * 8, i * 8 + 8)
            mid = mids[i]
            up = jnp.where(line == 0, pltpu.roll(column[i], 1, 0), pltpu.roll(mid, 1, 0))
            down = jnp.where(line == 7, pltpu.roll(column[i + 2], 7, 0), pltpu.roll(mid, 7, 0))
            next_left = jnp.where(tile == 0, 0.0, dif[rows, left])
            next_right = jnp.where(tile == TILES - 1, 0.0, dif[rows, right])
            west = jnp.where(first, pltpu.roll(next_left, 1, 1), pltpu.roll(mid, 1, 1))
            east = jnp.where(last, pltpu.roll(next_right, 127, 1), pltpu.roll(mid, 127, 1))
            sides = [0.1 * (mid + side) for side in (up, down, west, east)]
            for ref, side in zip((k_up, k_down, k_left, k_right), sides):
                ref[rows, here] = side
            keep[rows, here] = 1.0 - ((sides[0] + sides[1]) + (sides[2] + sides[3]))
            lv[rows, here] = lv[rows, here] * rate[rows, here]

    wide = 4

    def advance(now, content_now, later, content_later, row_tiles):

        @pl.loop(0, TILES // wide)
        def _(group):
            for row_tile in row_tiles:
                rows = slice(row_tile * 8, row_tile * 8 + 8)
                base = 8 + row_tile * 8
                heres = [
                    pl.ds(pl.multiple_of((group * wide + j) * 128, 128), 128) for j in range(wide)
                ]
                weights = [
                    [ref[rows, here] for ref in (keep, k_up, k_down, k_left, k_right, lp, lv, rate)]
                    for here in heres
                ]
                for m in range(OWN):
                    mids = [
                        now[group * wide + j, m, base : base + 8, :] for j in range(wide + 2)
                    ]
                    to_right = [pltpu.roll(mids[j], 1, 1) for j in range(wide + 1)]
                    to_left = [None] + [pltpu.roll(mids[j], 127, 1) for j in range(1, wide + 2)]
                    for j in range(wide):
                        keep_w, up_w, down_w, left_w, right_w, lp_w, lv_w, rate_w = weights[j]
                        tile = group * wide + j + 1
                        mid = mids[j + 1]
                        up = now[tile, m, base - 1 : base + 7, :]
                        down = now[tile, m, base + 1 : base + 9, :]
                        west = jnp.where(first, to_right[j], to_right[j + 1])
                        east = jnp.where(last, to_left[j + 2], to_left[j + 1])
                        content = content_now[m, rows, heres[j]]
                        inverse = pltpu.reciprocal(lp_w + jnp.abs(mid), approx=True)
                        release = rate_w * content - (lv_w * mid) * inverse
                        flow = (up_w * up + down_w * down) + (left_w * west + right_w * east)
                        later[tile, m, base : base + 8, :] = (
                            keep_w * mid + flow + release
                        )
                        content_later[m, rows, heres[j]] = content - release

    def one_step(step, now, content_now, later, content_later, flat_now, flat_later, more):
        advance(now, content_now, later, content_later, (1, 2))
        for i in range(2):
            halo_copy(step, i).wait()

        @pl.loop(0, TILES)
        def _(tile):
            top = jnp.where(at_top, 0.0, in_top[step, tile])
            low = jnp.where(at_low, 0.0, in_low[step, tile])
            flat_now[tile + 1, pl.ds(7, OWN, stride=PAD_ROWS), :] = top
            flat_now[tile + 1, pl.ds(8 + ROWS, OWN, stride=PAD_ROWS), :] = low

        advance(now, content_now, later, content_later, (0, 3))

        @pl.when(more)
        def _():
            send_halo(step + 1, flat_later)

    @pl.loop(0, STEPS // 2)
    def _(pair):
        one_step(2 * pair, p, c, p_other, c_other, flat, flat_other, True)
        one_step(2 * pair + 1, p_other, c_other, p, c, flat_other, flat, pair < STEPS // 2 - 1)

    store_c = pltpu.make_async_copy(c, c_out, c_sem)
    store_c.start()

    @pl.loop(1, PEERS)
    def _(i):
        cell_copy(i).wait()

    def to_blocks(target):
        for a in range(SIDE):
            index = jnp.broadcast_to(all_cells[target, a : a + 1, :], (OWN, 128))
            observed = jnp.zeros((OWN, 128), jnp.float32)
            for j in range(2):
                lines = [
                    flat[target * 2 + j + 1, pl.ds(8 + a * BR + r, OWN, stride=PAD_ROWS), :]
                    for r in range(BR)
                ]
                blocks = swap_groups(lines)
                for b in range(4):
                    send[target, a * SIDE + j * 4 + b] = blocks[b]
                    picked = jnp.take_along_axis(blocks[b], index, axis=1)
                    observed = jnp.where(slot_group == j * 4 + b, picked, observed)
            obs_send[target, a] = observed

    mine = pl.ds(pl.multiple_of(mem * OWN, OWN), OWN)

    def obs_copy(i):
        target = lax.rem(mem + i, PEERS)
        return pltpu.make_async_remote_copy(
            src_ref=obs_send.at[target], dst_ref=obs_in.at[:, mine, :],
            send_sem=obs_send_sem.at[i], recv_sem=obs_recv_sem.at[i],
            device_id=(target, slab), device_id_type=mesh_ids,
        )

    def block_copy(part, i):
        way = ways[i]
        target = lax.rem(mem // 4 + way[0], 4) * 4 + lax.rem(mem + way[1], 4)
        blocks = pl.ds(part * 2 * SIDE, 2 * SIDE)
        return pltpu.make_async_remote_copy(
            src_ref=send.at[target, blocks], dst_ref=gathered.at[blocks, mine, :],
            send_sem=send_sem.at[part, i], recv_sem=recv_sem.at[part, i],
            device_id=(target, slab), device_id_type=mesh_ids,
        )

    @pl.loop(1, PEERS)
    def _(i):
        to_blocks(lax.rem(mem + i, PEERS))
        obs_copy(i).start()

    to_blocks(mem)
    for i in range(len(ways)):
        block_copy(0, i).start()
    own = pltpu.make_async_copy(send.at[mem], gathered.at[:, mine, :], own_sem.at[0])
    own.start()
    own_obs = pltpu.make_async_copy(obs_send.at[mem], obs_in.at[:, mine, :], own_sem.at[1])
    own_obs.start()
    own_obs.wait()

    @pl.loop(1, PEERS)
    def _(i):
        obs_copy(i).wait()

    @pl.loop(0, SIDE)
    def _(a):
        seen = obs_in[a]
        centre = jnp.mean(seen, axis=0, keepdims=True)
        root = roots[pl.ds(a, 1), :]
        spread = ((seen - centre) * root).T
        innovation = jnp.broadcast_to((values[pl.ds(a, 1), :] - centre) * root, (128, 128)).T
        for b in range(SIDE):
            obs_pad[a + 1, b + 1, 0:OBS_MAX, :] = spread[b * OBS_MAX : (b + 1) * OBS_MAX]
            obs_pad[a + 1, b + 1, OBS_MAX:, :] = innovation[b * OBS_MAX : (b + 1) * OBS_MAX]

    def side_copy(i):
        src, dst, device = (
            (obs_pad.at[1:9, 8], obs_pad.at[1:9, 0], (lax.rem(mem + 1, PEERS), slab)),
            (obs_pad.at[1:9, 1], obs_pad.at[1:9, 9], (lax.rem(mem + PEERS - 1, PEERS), slab)),
            (obs_pad.at[8], obs_pad.at[0], (mem, below)),
            (obs_pad.at[1], obs_pad.at[9], (mem, above)),
        )[i]
        return pltpu.make_async_remote_copy(
            src_ref=src, dst_ref=dst, send_sem=side_send.at[i], recv_sem=side_recv.at[i],
            device_id=device, device_id_type=mesh_ids,
        )

    blank = jnp.zeros((2 * OBS_MAX, 128), jnp.float32)
    for sides, conditions in (
        ((0, 1), (mem == 0, mem == PEERS - 1)),
        ((2, 3), (at_top, at_low)),
    ):
        for i in sides:
            side_copy(i).start()
        for i in sides:
            side_copy(i).wait()
        if sides[0] == 0:

            @pl.loop(1, PARTS)
            def _(part):
                for i in range(len(ways)):
                    block_copy(part, i).start()

        for i, condition in zip(sides, conditions):

            @pl.when(condition)
            def _(i=i):
                @pl.loop(*((1, SIDE + 1) if i < 2 else (0, SIDE + 2)))
                def _(place):
                    if i < 2:
                        obs_pad[place, 0 if i == 0 else SIDE + 1] = blank
                    else:
                        obs_pad[0 if i == 2 else SIDE + 1, place] = blank

    half_lane = lax.broadcasted_iota(jnp.int32, (1, 128), 1) < HALF
    diagonal = lax.broadcasted_iota(jnp.int32, (HALF, 128), 0) == lax.rem(
        lax.broadcasted_iota(jnp.int32, (HALF, 128), 1), HALF
    )
    pair_eye = jnp.where(diagonal, 1.0, 0.0)
    eye = lax.broadcasted_iota(jnp.int32, (128, 128), 0) == lax.broadcasted_iota(
        jnp.int32, (128, 128), 1
    )
    no_rows = jnp.zeros((HALF, 128), jnp.float32)

    @pl.loop(0, BLOCKS // (2 * PAIRS))
    def _(group):
        start = []
        for pair in range(PAIRS):
            for i in range(2 * NBR):
                place = 2 * pair + i // NBR
                a = group * (PAIRS // 4) + place // SIDE
                b = place % SIDE
                code = neighbour[a, b, i % NBR]
                down_by = lax.div(code, 3)
                right_by = code - 3 * down_by
                block = obs_pad[a + down_by, b + right_by]
                far = (down_by != 1).astype(jnp.int32) + (right_by != 1).astype(jnp.int32)
                weight = jnp.where(
                    far == 0, 1.0, jnp.where(far == 1, side_weight, corner_weight)
                )
                rows_z[pair, i * OBS_MAX : (i + 1) * OBS_MAX, :] = weight * block[:OBS_MAX]
                innov_z[pair, i * OBS_MAX : (i + 1) * OBS_MAX, :] = weight * block[OBS_MAX:]
        rows = [rows_z[pair] for pair in range(PAIRS)]
        grams = [product(z, *split(z.T)) for z in rows]
        smalls = [jnp.where(half_lane, gram[:HALF], gram[HALF:]) for gram in grams]
        traces = [
            jnp.sum(jnp.where(diagonal, small, 0.0), axis=0, keepdims=True) for small in smalls
        ]
        totals = [
            [
                MEMBERS * ridge + jnp.sum(jnp.where(side, trace, 0.0), axis=1, keepdims=True)
                for side in (half_lane, jnp.logical_not(half_lane))
            ]
            for trace in traces
        ]
        for pair, (small, total) in enumerate(zip(smalls, totals)):
            scale = 1.0 / jnp.where(half_lane, total[0], total[1])
            low = ridge * scale
            now_x[pair] = small * scale + low * pair_eye
            now_m[pair] = no_rows
            now_d[pair] = pair_eye
            start.append((low, jnp.ones_like(low)))

        def sweep(_, carry):
            states = [(now_x[i], now_m[i], now_d[i]) for i in range(PAIRS)]
            by_x = [
                pair_product(jnp.concatenate(state, axis=0), state[0]) for state in states
            ]
            factors = [
                0.25 * result[:HALF] - 1.5 * state[0] + 2.25 * pair_eye
                for result, state in zip(by_x, states)
            ]
            by_f = [
                pair_product(jnp.concatenate([x, d], axis=0), factor)
                for (x, _, d), factor in zip(states, factors)
            ]
            ahead = []
            later = []
            for (x, m, d), (low, gain), first, second in zip(states, carry, by_x, by_f):
                new_d = (
                    second[HALF:]
                    + (0.25 * low) * first[2 * HALF :]
                    + (0.25 * low * (low - 6.0)) * d
                )
                new_m = 1.5 * m - 0.5 * first[HALF : 2 * HALF] - (0.5 * gain) * d
                later.append((second[:HALF], new_m, new_d))
                shrink = 1.5 - 0.5 * low
                ahead.append((low * shrink * shrink, gain * shrink))
            for i in range(PAIRS):
                now_x[i], now_m[i], now_d[i] = later[i]
            return tuple(ahead)

        last_low = lax.fori_loop(0, NS_ITERS - 1, sweep, tuple(start))
        states = [(now_x[i], now_m[i], now_d[i]) for i in range(PAIRS)]
        rows = [rows_z[pair] for pair in range(PAIRS)]
        by_x = [pair_product(m, x) for x, m, _ in states]
        ends = []
        for (_, m, d), (_, gain), total, result in zip(states, last_low, totals, by_x):
            both = jnp.where(half_lane, total[0], total[1])
            m = 1.5 * m - 0.5 * result - (0.5 * gain) * d
            m = m * (1.0 / (both * jnp.sqrt(both)))
            ends.append(
                jnp.concatenate(
                    [jnp.where(half_lane, m, 0.0), jnp.where(half_lane, 0.0, m)], axis=0
                )
            )
        by_z = [product(end, *split(z)) for end, z in zip(ends, rows)]
        wide_z = [
            jnp.concatenate(
                [
                    jnp.concatenate([m_z[:HALF], no_rows], axis=0),
                    jnp.concatenate([no_rows, m_z[HALF:]], axis=0),
                ],
                axis=1,
            )
            for m_z in by_z
        ]
        roots_both = [product(z.T, *split(right)) for z, right in zip(rows, wide_z)]
        gains = []
        pulls = []
        for pair, (z, total) in enumerate(zip(rows, totals)):
            for side in range(2):
                low = ridge / total[side]
                gain = 1.0 / jnp.sqrt(total[side])
                for _ in range(NS_ITERS):
                    shrink = 1.5 - 0.5 * low
                    low, gain = low * shrink * shrink, gain * shrink
                gains.append(gain)
                own_rows = slice(side * HALF, side * HALF + HALF)
                pulls.append(
                    jnp.sum(innov_z[pair, own_rows] * z[own_rows], axis=0, keepdims=True)
                )
        for i, (gain, pull) in enumerate(zip(gains, pulls)):
            column = i % 2 * 128
            root = roots_both[i // 2][:, column : column + 128] + jnp.where(eye, gain, 0.0)
            first_pass = jnp.sum(root * pull, axis=1, keepdims=True)
            shift = jnp.sum(root * first_pass, axis=0, keepdims=True)
            weights_now[group * 2 * PAIRS + i] = member_root * root + shift

    flat_lines = lines.reshape(PARTS, 2, MEMBERS * 8, 128)

    def out_copy(part, j):
        return pltpu.make_async_copy(
            lines.at[part, j],
            analysis.at[:, pl.ds(pl.multiple_of(part * 8, 8), 8), pl.ds(j * 128, 128)],
            out_sem.at[part, j],
        )

    own.wait()

    @pl.loop(0, PARTS)
    def _(part):
        for i in range(len(ways)):
            block_copy(part, i).wait()

        @pl.loop(0, 2)
        def _(a):
            places = [part * 2 * SIDE + a * SIDE + b for b in range(SIDE)]
            fields = [gathered[place] for place in places]
            centres = [jnp.mean(field, axis=0, keepdims=True) for field in fields]
            updated = [
                product(weights_now[place], *split(field - centre)) + centre
                for place, field, centre in zip(places, fields, centres)
            ]
            for j in range(2):
                for m in range(MEMBERS // 8):
                    rows = swap_groups(
                        [block[m * 8 : m * 8 + 8] for block in updated[4 * j : 4 * j + 4]]
                    )
                    for r in range(BR):
                        at = pl.ds(m * 64 + a * BR + r, 8, stride=8)
                        flat_lines[part, j, at, :] = rows[r]

        for j in range(2):
            out_copy(part, j).start()

    @pl.loop(0, PARTS)
    def _(part):
        for j in range(2):
            out_copy(part, j).wait()

    store_c.wait()


def assimilate(*arguments):
    field = (ROWS, COLS)
    f32 = jnp.float32
    anywhere = pl.BlockSpec(memory_space=pl.ANY)
    local = pl.BlockSpec(memory_space=pltpu.VMEM)
    halo = pltpu.VMEM((STEPS, TILES, OWN, 128), f32)
    dma = pltpu.SemaphoreType.DMA
    square = pltpu.VMEM((BLOCKS, MEMBERS, 128), f32)
    return pl.pallas_call(
        assimilate_kernel,
        out_shape=(
            jax.ShapeDtypeStruct((MEMBERS, ROWS, 2 * 128), f32),
            jax.ShapeDtypeStruct((OWN, ROWS, COLS), f32),
        ),
        in_specs=[anywhere] * 6 + [local] * 4 + [pl.BlockSpec(memory_space=pltpu.SMEM)],
        out_specs=[anywhere] * 2,
        scratch_shapes=[
            *[pltpu.VMEM((TILES + 2, OWN, PAD_ROWS, 128), f32)] * 2,
            *[pltpu.VMEM((OWN, ROWS, COLS), f32)] * 2,
            *[pltpu.VMEM(field, f32)] * 4,
            *[pltpu.VMEM((8, COLS), f32)] * 2,
            *[pltpu.VMEM(field, f32)] * 5,
            *[halo] * 4,
            pltpu.VMEM((PEERS, BLOCKS, OWN, 128), f32),
            pltpu.VMEM((SIDE, 128), jnp.int32),
            *[pltpu.VMEM((SIDE, 128), f32)] * 2,
            pltpu.VMEM((PEERS, SIDE, 128), jnp.int32),
            pltpu.VMEM((PEERS, SIDE, OWN, 128), f32),
            pltpu.VMEM((SIDE, MEMBERS, 128), f32),
            pltpu.VMEM((SIDE + 2, SIDE + 2, 2 * OBS_MAX, 128), f32),
            *[pltpu.VMEM((PAIRS, 2 * HALF, 128), f32)] * 2,
            *[pltpu.VMEM((PAIRS, HALF, 128), f32)] * 3,
            square, square,
            pltpu.VMEM((PARTS, 2, MEMBERS, 8, 128), f32),
            dma((5,)), dma((TILES,)), dma((2,)), dma((2,)),
            dma((STEPS, 2)), dma((STEPS, 2)), dma((PARTS, PEERS)), dma((PARTS, PEERS)),
            dma((2,)), dma,
            dma((PEERS,)), dma((PEERS,)), dma((PEERS,)), dma((PEERS,)), dma((4,)), dma((4,)),
            dma((PARTS, 2)),
        ],
        compiler_params=pltpu.CompilerParams(
            collective_id=0, has_side_effects=True, vmem_limit_bytes=62 << 20
        ),
        name="assimilate",
    )(*arguments)


def solution(mesh):
    placed = (
        P("mem", "slab", None),
        P("mem", "slab", None),
        P("slab", None),
        P("slab", None),
        P("slab", None),
        P("slab", None),
        P("slab", "mem", None),
        P("slab", "mem", None),
        P("slab", "mem", None),
        P("slab", "mem"),
        P("slab", "mem", None),
    )
    return jax.shard_map(
        assimilate,
        mesh=mesh,
        in_specs=placed,
        out_specs=(P(None, "slab", "mem"), P("mem", "slab", None)),
        check_vma=False,
    )
```

```python
import math

import jax
import jax.numpy as jnp
from jax import lax
from jax.experimental import pallas as pl
from jax.experimental.pallas import tpu as pltpu
from jax.sharding import PartitionSpec as P

MEMBERS = 128
STEPS = 4
BR = 4
BC = 32
OBS_MAX = 16
NBR = 4
NS_ITERS = 7

PEERS = 16
SLABS = 8
OWN = 8
ROWS = 32
COLS = 4096
TILES = 32
PAD_ROWS = 48
BLOCKS = 64
SIDE = 8
PAIRS = 8
PARTS = 4
HALF = NBR * OBS_MAX

inflation = 1.1
ridge = (MEMBERS - 1) / inflation
member_root = math.sqrt(MEMBERS - 1)
side_weight = math.exp(-0.25)
corner_weight = math.exp(-0.5)
mesh_ids = pl.DeviceIdType.MESH

ways = (
    (1, 0), (3, 0), (2, 2), (0, 2), (2, 0), (1, 1), (3, 3), (1, 3), (3, 1), (2, 1), (1, 2),
    (2, 3), (3, 2), (0, 1), (0, 3),
)


def split(value):
    head = value.astype(jnp.bfloat16)
    return head, (value - head.astype(jnp.float32)).astype(jnp.bfloat16)


def product(left, head, tail):
    left_head, left_tail = split(left)
    both = jnp.concatenate([head, tail], axis=1)
    result = jnp.dot(
        jnp.concatenate([left_head, left_tail], axis=1),
        jnp.concatenate([both, both], axis=0),
        preferred_element_type=jnp.float32,
    )
    columns = head.shape[1]
    return result[:, :columns] + result[:, columns:]


def pair_product(left, right):
    same = (lax.broadcasted_iota(jnp.int32, (128, 128), 0) < HALF) == (
        lax.broadcasted_iota(jnp.int32, (128, 128), 1) < HALF
    )
    head, tail = (
        jnp.where(same, jnp.concatenate([part, part], axis=0), jnp.zeros((128, 128), jnp.bfloat16))
        for part in split(right)
    )
    return product(left, head, tail)


def swap_groups(rows):
    group = lax.broadcasted_iota(jnp.int32, (8, 128), 1) // BC
    even = group % 2 == 0
    low = group < 2
    near = [None] * 4
    for i in (0, 2):
        near[i] = jnp.where(even, rows[i], pltpu.roll(rows[i + 1], BC, 1))
        near[i + 1] = jnp.where(even, pltpu.roll(rows[i], 128 - BC, 1), rows[i + 1])
    out = [None] * 4
    for i in (0, 1):
        out[i] = jnp.where(low, near[i], pltpu.roll(near[i + 2], 64, 1))
        out[i + 2] = jnp.where(low, pltpu.roll(near[i], 64, 1), near[i + 2])
    return out


def assimilate_kernel(
    p_in, c_in, d_in, lp_in, lv_in, rate_in, cell_in, value_in, error_in, count_in, neighbour,
    analysis, c_out,
    p, p_other, c, c_other, lp, lv, rate, dif, dif_top, dif_low, keep, k_up, k_down, k_left, k_right,
    out_up, out_down, in_top, in_low, send,
    cells, values, roots, all_cells, obs_send, obs_in, obs_pad,
    rows_z, innov_z, now_x, now_m, now_d, weights_now, gathered, lines,
    load_sem, p_sem, dif_send, dif_recv, halo_send, halo_recv, send_sem, recv_sem, own_sem, c_sem,
    cell_send, cell_recv, obs_send_sem, obs_recv_sem, side_send, side_recv, out_sem,
):
    mem = lax.axis_index("mem")
    slab = lax.axis_index("slab")
    above = lax.rem(slab + SLABS - 1, SLABS)
    below = lax.rem(slab + 1, SLABS)

    def load_p(tile):
        return pltpu.make_async_copy(
            p_in.at[:, :, pl.ds(pl.multiple_of(tile * 128, 128), 128)],
            p.at[tile + 1, :, pl.ds(8, ROWS), :],
            p_sem.at[tile],
        )

    loads = [
        pltpu.make_async_copy(src, dst, load_sem.at[i])
        for i, (src, dst) in enumerate(
            ((d_in, dif), (lp_in, lp), (lv_in, lv), (rate_in, rate), (c_in, c))
        )
    ]
    for load in loads[:1]:
        load.start()

    @pl.loop(0, TILES)
    def _(tile):
        load_p(tile).start()

    for load in loads[1:]:
        load.start()

    lane = lax.broadcasted_iota(jnp.int32, (8, 128), 1)
    line = lax.broadcasted_iota(jnp.int32, (8, 128), 0)
    slot_group = lane // OBS_MAX

    def lay_out(piece_of):
        out = piece_of(0)
        for b in range(1, SIDE):
            out = jnp.where(slot_group == b, piece_of(b), out)
        return out

    def slots_of(ref):
        return lay_out(lambda b: jnp.concatenate([ref[:, b, :]] * SIDE, axis=1))

    cells[...] = slots_of(cell_in)
    values[...] = slots_of(value_in)
    counts = lay_out(lambda b: jnp.broadcast_to(count_in[:, b : b + 1], (SIDE, 128)))
    live = lax.rem(lane, OBS_MAX) < counts
    roots[...] = jnp.where(live, jnp.sqrt(slots_of(error_in)), 0.0)

    barrier = pltpu.get_barrier_semaphore()

    @pl.loop(1, PEERS)
    def _(i):
        pl.semaphore_signal(
            barrier, inc=1, device_id=(lax.rem(mem + i, PEERS), slab),
            device_id_type=pl.DeviceIdType.MESH,
        )

    for other in (above, below):
        pl.semaphore_signal(
            barrier, inc=1, device_id=(mem, other), device_id_type=pl.DeviceIdType.MESH
        )

    zero = jnp.zeros((8, 128), jnp.float32)
    for field in (p, p_other):
        for tile in (0, TILES + 1):
            for m in range(OWN):
                for i in range(PAD_ROWS // 8):
                    field[tile, m, i * 8 : i * 8 + 8, :] = zero

    pl.semaphore_wait(barrier, PEERS + 1)

    def dif_copy(i, src, dst, other):
        return pltpu.make_async_remote_copy(
            src_ref=src, dst_ref=dst, send_sem=dif_send.at[i], recv_sem=dif_recv.at[i],
            device_id=(mem, other), device_id_type=pl.DeviceIdType.MESH,
        )

    def cell_copy(i):
        return pltpu.make_async_remote_copy(
            src_ref=cells, dst_ref=all_cells.at[mem],
            send_sem=cell_send.at[i], recv_sem=cell_recv.at[i],
            device_id=(lax.rem(mem + i, PEERS), slab), device_id_type=mesh_ids,
        )

    @pl.loop(1, PEERS)
    def _(i):
        cell_copy(i).start()

    all_cells[mem] = cells[...]

    dif_copies = [
        dif_copy(0, d_in.at[pl.ds(24, 8)], dif_top, below),
        dif_copy(1, d_in.at[pl.ds(0, 8)], dif_low, above),
    ]
    for copy in dif_copies:
        copy.start()

    def halo_copy(step, i):
        src, dst, other = ((out_down, in_top, below), (out_up, in_low, above))[i]
        return pltpu.make_async_remote_copy(
            src_ref=src.at[step], dst_ref=dst.at[step],
            send_sem=halo_send.at[step, i], recv_sem=halo_recv.at[step, i],
            device_id=(mem, other), device_id_type=pl.DeviceIdType.MESH,
        )

    flat, flat_other = (
        field.reshape(TILES + 2, OWN * PAD_ROWS, 128) for field in (p, p_other)
    )

    def send_halo(step):
        for i in range(2):
            halo_copy(step, i).start()

    first_row = pl.ds(8, OWN, stride=PAD_ROWS)
    last_row = pl.ds(7 + ROWS, OWN, stride=PAD_ROWS)

    def clear_outside(field, tile):
        field[tile + 1, pl.ds(7, OWN, stride=PAD_ROWS), :] = zero
        field[tile + 1, pl.ds(8 + ROWS, OWN, stride=PAD_ROWS), :] = zero

    @pl.loop(0, TILES, unroll=8)
    def _(tile):
        clear_outside(flat_other, tile)

    @pl.loop(0, TILES)
    def _(tile):
        load_p(tile).wait()

    @pl.loop(0, TILES, unroll=8)
    def _(tile):
        clear_outside(flat, tile)
        out_up[0, tile] = flat[tile + 1, first_row, :]
        out_down[0, tile] = flat[tile + 1, last_row, :]

    send_halo(0)

    for load in loads:
        load.wait()
    for copy in dif_copies:
        copy.wait()

    first, last = lane == 0, lane == 127
    at_top, at_low = slab == 0, slab == SLABS - 1

    @pl.loop(0, TILES, unroll=4)
    def _(tile):
        here = pl.ds(pl.multiple_of(tile * 128, 128), 128)
        left = pl.ds(pl.multiple_of(jnp.maximum(tile - 1, 0) * 128, 128), 128)
        right = pl.ds(pl.multiple_of(jnp.minimum(tile + 1, TILES - 1) * 128, 128), 128)
        top_row = jnp.where(at_top, 0.0, dif_top[:, here])
        low_row = jnp.where(at_low, 0.0, dif_low[:, here])
        mids = [dif[i * 8 : i * 8 + 8, here] for i in range(4)]
        column = [top_row, *mids, low_row]
        for i in range(4):
            rows = slice(i * 8, i * 8 + 8)
            mid = mids[i]
            up = jnp.where(line == 0, pltpu.roll(column[i], 1, 0), pltpu.roll(mid, 1, 0))
            down = jnp.where(line == 7, pltpu.roll(column[i + 2], 7, 0), pltpu.roll(mid, 7, 0))
            next_left = jnp.where(tile == 0, 0.0, dif[rows, left])
            next_right = jnp.where(tile == TILES - 1, 0.0, dif[rows, right])
            west = jnp.where(first, pltpu.roll(next_left, 1, 1), pltpu.roll(mid, 1, 1))
            east = jnp.where(last, pltpu.roll(next_right, 127, 1), pltpu.roll(mid, 127, 1))
            sides = [0.1 * (mid + side) for side in (up, down, west, east)]
            for ref, side in zip((k_up, k_down, k_left, k_right), sides):
                ref[rows, here] = side
            keep[rows, here] = 1.0 - ((sides[0] + sides[1]) + (sides[2] + sides[3]))
            lv[rows, here] = lv[rows, here] * rate[rows, here]

    wide = 4

    def advance(now, content_now, later, content_later):

        @pl.loop(0, TILES // wide)
        def _(group):
            for row_tile in range(ROWS // 8):
                rows = slice(row_tile * 8, row_tile * 8 + 8)
                base = 8 + row_tile * 8
                heres = [
                    pl.ds(pl.multiple_of((group * wide + j) * 128, 128), 128) for j in range(wide)
                ]
                weights = [
                    [ref[rows, here] for ref in (keep, k_up, k_down, k_left, k_right, lp, lv, rate)]
                    for here in heres
                ]
                for m in range(OWN):
                    mids = [
                        now[group * wide + j, m, base : base + 8, :] for j in range(wide + 2)
                    ]
                    to_right = [pltpu.roll(mids[j], 1, 1) for j in range(wide + 1)]
                    to_left = [None] + [pltpu.roll(mids[j], 127, 1) for j in range(1, wide + 2)]
                    for j in range(wide):
                        keep_w, up_w, down_w, left_w, right_w, lp_w, lv_w, rate_w = weights[j]
                        tile = group * wide + j + 1
                        mid = mids[j + 1]
                        up = now[tile, m, base - 1 : base + 7, :]
                        down = now[tile, m, base + 1 : base + 9, :]
                        west = jnp.where(first, to_right[j], to_right[j + 1])
                        east = jnp.where(last, to_left[j + 2], to_left[j + 1])
                        content = content_now[m, rows, heres[j]]
                        inverse = pltpu.reciprocal(lp_w + jnp.abs(mid), approx=True)
                        release = rate_w * content - (lv_w * mid) * inverse
                        flow = (up_w * up + down_w * down) + (left_w * west + right_w * east)
                        later[tile, m, base : base + 8, :] = (
                            keep_w * mid + flow + release
                        )
                        content_later[m, rows, heres[j]] = content - release

    def one_step(step, now, content_now, later, content_later, flat_later, more):
        advance(now, content_now, later, content_later)
        for i in range(2):
            halo_copy(step, i).wait()
        following = lax.rem(step + 1, STEPS)

        @pl.loop(0, TILES, unroll=8)
        def _(tile):
            here = pl.ds(pl.multiple_of(tile * 128, 128), 128)
            top = jnp.where(at_top, 0.0, in_top[step, tile]) * k_up[0:1, here]
            low = jnp.where(at_low, 0.0, in_low[step, tile]) * k_down[ROWS - 1 : ROWS, here]
            top = flat_later[tile + 1, first_row, :] + top
            low = flat_later[tile + 1, last_row, :] + low
            flat_later[tile + 1, first_row, :] = top
            flat_later[tile + 1, last_row, :] = low
            out_up[following, tile] = top
            out_down[following, tile] = low

        @pl.when(more)
        def _():
            send_halo(step + 1)

    @pl.loop(0, STEPS // 2)
    def _(pair):
        one_step(2 * pair, p, c, p_other, c_other, flat_other, True)
        one_step(2 * pair + 1, p_other, c_other, p, c, flat, pair < STEPS // 2 - 1)

    store_c = pltpu.make_async_copy(c, c_out, c_sem)
    store_c.start()

    @pl.loop(1, PEERS)
    def _(i):
        cell_copy(i).wait()

    def to_blocks(target):
        for a in range(SIDE):
            index = jnp.broadcast_to(all_cells[target, a : a + 1, :], (OWN, 128))
            observed = jnp.zeros((OWN, 128), jnp.float32)
            for j in range(2):
                lines = [
                    flat[target * 2 + j + 1, pl.ds(8 + a * BR + r, OWN, stride=PAD_ROWS), :]
                    for r in range(BR)
                ]
                blocks = swap_groups(lines)
                for b in range(4):
                    send[target, a * SIDE + j * 4 + b] = blocks[b]
                    picked = jnp.take_along_axis(blocks[b], index, axis=1)
                    observed = jnp.where(slot_group == j * 4 + b, picked, observed)
            obs_send[target, a] = observed

    mine = pl.ds(pl.multiple_of(mem * OWN, OWN), OWN)

    def place_of(code):
        return lax.rem(mem // 4 + code // 4, 4) * 4 + lax.rem(mem + code, 4)

    def obs_copy(i):
        target = place_of(i)
        return pltpu.make_async_remote_copy(
            src_ref=obs_send.at[target], dst_ref=obs_in.at[:, mine, :],
            send_sem=obs_send_sem.at[i], recv_sem=obs_recv_sem.at[i],
            device_id=(target, slab), device_id_type=mesh_ids,
        )

    def block_copy(part, i):
        target = place_of(i)
        blocks = pl.ds(part * 2 * SIDE, 2 * SIDE)
        return pltpu.make_async_remote_copy(
            src_ref=send.at[target, blocks], dst_ref=gathered.at[blocks, mine, :],
            send_sem=send_sem.at[part, i], recv_sem=recv_sem.at[part, i],
            device_id=(target, slab), device_id_type=mesh_ids,
        )

    @pl.loop(1, PEERS)
    def _(i):
        code = lax.rem(7 * i, PEERS)
        to_blocks(place_of(code))
        obs_copy(code).start()
        block_copy(0, code).start()

    to_blocks(mem)
    own = pltpu.make_async_copy(send.at[mem], gathered.at[:, mine, :], own_sem.at[0])
    own.start()
    own_obs = pltpu.make_async_copy(obs_send.at[mem], obs_in.at[:, mine, :], own_sem.at[1])
    own_obs.start()
    own_obs.wait()

    @pl.loop(1, PEERS)
    def _(i):
        obs_copy(i).wait()

    @pl.loop(0, SIDE)
    def _(a):
        seen = obs_in[a]
        centre = jnp.mean(seen, axis=0, keepdims=True)
        root = roots[pl.ds(a, 1), :]
        spread = ((seen - centre) * root).T
        innovation = jnp.broadcast_to((values[pl.ds(a, 1), :] - centre) * root, (128, 128)).T
        for b in range(SIDE):
            obs_pad[a + 1, b + 1, 0:OBS_MAX, :] = spread[b * OBS_MAX : (b + 1) * OBS_MAX]
            obs_pad[a + 1, b + 1, OBS_MAX:, :] = innovation[b * OBS_MAX : (b + 1) * OBS_MAX]

    def side_copy(i):
        src, dst, device = (
            (obs_pad.at[1:9, 8], obs_pad.at[1:9, 0], (lax.rem(mem + 1, PEERS), slab)),
            (obs_pad.at[1:9, 1], obs_pad.at[1:9, 9], (lax.rem(mem + PEERS - 1, PEERS), slab)),
            (obs_pad.at[8], obs_pad.at[0], (mem, below)),
            (obs_pad.at[1], obs_pad.at[9], (mem, above)),
        )[i]
        return pltpu.make_async_remote_copy(
            src_ref=src, dst_ref=dst, send_sem=side_send.at[i], recv_sem=side_recv.at[i],
            device_id=device, device_id_type=mesh_ids,
        )

    blank = jnp.zeros((2 * OBS_MAX, 128), jnp.float32)
    for sides, conditions in (
        ((0, 1), (mem == 0, mem == PEERS - 1)),
        ((2, 3), (at_top, at_low)),
    ):
        for i in sides:
            side_copy(i).start()
        for i in sides:
            side_copy(i).wait()
        if sides[0] == 0:

            @pl.loop(1, PARTS)
            def _(part):
                for way in ways:
                    block_copy(part, 4 * way[0] + way[1]).start()

        for i, condition in zip(sides, conditions):

            @pl.when(condition)
            def _(i=i):
                @pl.loop(*((1, SIDE + 1) if i < 2 else (0, SIDE + 2)))
                def _(place):
                    if i < 2:
                        obs_pad[place, 0 if i == 0 else SIDE + 1] = blank
                    else:
                        obs_pad[0 if i == 2 else SIDE + 1, place] = blank

    half_lane = lax.broadcasted_iota(jnp.int32, (1, 128), 1) < HALF
    diagonal = lax.broadcasted_iota(jnp.int32, (HALF, 128), 0) == lax.rem(
        lax.broadcasted_iota(jnp.int32, (HALF, 128), 1), HALF
    )
    pair_eye = jnp.where(diagonal, 1.0, 0.0)
    eye = lax.broadcasted_iota(jnp.int32, (128, 128), 0) == lax.broadcasted_iota(
        jnp.int32, (128, 128), 1
    )
    no_rows = jnp.zeros((HALF, 128), jnp.float32)

    @pl.loop(0, BLOCKS // (2 * PAIRS))
    def _(group):
        start = []
        for pair in range(PAIRS):
            for i in range(2 * NBR):
                place = 2 * pair + i // NBR
                a = group * (PAIRS // 4) + place // SIDE
                b = place % SIDE
                code = neighbour[a, b, i % NBR]
                down_by = lax.div(code, 3)
                right_by = code - 3 * down_by
                block = obs_pad[a + down_by, b + right_by]
                far = (down_by != 1).astype(jnp.int32) + (right_by != 1).astype(jnp.int32)
                weight = jnp.where(
                    far == 0, 1.0, jnp.where(far == 1, side_weight, corner_weight)
                )
                rows_z[pair, i * OBS_MAX : (i + 1) * OBS_MAX, :] = weight * block[:OBS_MAX]
                innov_z[pair, i * OBS_MAX : (i + 1) * OBS_MAX, :] = weight * block[OBS_MAX:]
        rows = [rows_z[pair] for pair in range(PAIRS)]
        grams = [product(z, *split(z.T)) for z in rows]
        smalls = [jnp.where(half_lane, gram[:HALF], gram[HALF:]) for gram in grams]
        traces = [
            jnp.sum(jnp.where(diagonal, small, 0.0), axis=0, keepdims=True) for small in smalls
        ]
        totals = [
            [
                MEMBERS * ridge + jnp.sum(jnp.where(side, trace, 0.0), axis=1, keepdims=True)
                for side in (half_lane, jnp.logical_not(half_lane))
            ]
            for trace in traces
        ]
        for pair, (small, total) in enumerate(zip(smalls, totals)):
            scale = 1.0 / jnp.where(half_lane, total[0], total[1])
            low = ridge * scale
            now_x[pair] = small * scale + low * pair_eye
            now_m[pair] = no_rows
            now_d[pair] = pair_eye
            start.append((low, jnp.ones_like(low)))

        def sweep(_, carry):
            states = [(now_x[i], now_m[i], now_d[i]) for i in range(PAIRS)]
            by_x = [
                pair_product(jnp.concatenate(state, axis=0), state[0]) for state in states
            ]
            factors = [
                0.25 * result[:HALF] - 1.5 * state[0] + 2.25 * pair_eye
                for result, state in zip(by_x, states)
            ]
            by_f = [
                pair_product(jnp.concatenate([x, d], axis=0), factor)
                for (x, _, d), factor in zip(states, factors)
            ]
            ahead = []
            later = []
            for (x, m, d), (low, gain), first, second in zip(states, carry, by_x, by_f):
                new_d = (
                    second[HALF:]
                    + (0.25 * low) * first[2 * HALF :]
                    + (0.25 * low * (low - 6.0)) * d
                )
                new_m = 1.5 * m - 0.5 * first[HALF : 2 * HALF] - (0.5 * gain) * d
                later.append((second[:HALF], new_m, new_d))
                shrink = 1.5 - 0.5 * low
                ahead.append((low * shrink * shrink, gain * shrink))
            for i in range(PAIRS):
                now_x[i], now_m[i], now_d[i] = later[i]
            return tuple(ahead)

        last_low = lax.fori_loop(0, NS_ITERS - 1, sweep, tuple(start))
        states = [(now_x[i], now_m[i], now_d[i]) for i in range(PAIRS)]
        rows = [rows_z[pair] for pair in range(PAIRS)]
        by_x = [pair_product(m, x) for x, m, _ in states]
        ends = []
        for (_, m, d), (_, gain), total, result in zip(states, last_low, totals, by_x):
            both = jnp.where(half_lane, total[0], total[1])
            m = 1.5 * m - 0.5 * result - (0.5 * gain) * d
            m = m * (1.0 / (both * jnp.sqrt(both)))
            ends.append(
                jnp.concatenate(
                    [jnp.where(half_lane, m, 0.0), jnp.where(half_lane, 0.0, m)], axis=0
                )
            )
        by_z = [product(end, *split(z)) for end, z in zip(ends, rows)]
        wide_z = [
            jnp.concatenate(
                [
                    jnp.concatenate([m_z[:HALF], no_rows], axis=0),
                    jnp.concatenate([no_rows, m_z[HALF:]], axis=0),
                ],
                axis=1,
            )
            for m_z in by_z
        ]
        roots_both = [product(z.T, *split(right)) for z, right in zip(rows, wide_z)]
        gains = []
        pulls = []
        for pair, (z, total) in enumerate(zip(rows, totals)):
            for side in range(2):
                low = ridge / total[side]
                gain = 1.0 / jnp.sqrt(total[side])
                for _ in range(NS_ITERS):
                    shrink = 1.5 - 0.5 * low
                    low, gain = low * shrink * shrink, gain * shrink
                gains.append(gain)
                own_rows = slice(side * HALF, side * HALF + HALF)
                pulls.append(
                    jnp.sum(innov_z[pair, own_rows] * z[own_rows], axis=0, keepdims=True)
                )
        for i, (gain, pull) in enumerate(zip(gains, pulls)):
            column = i % 2 * 128
            root = roots_both[i // 2][:, column : column + 128] + jnp.where(eye, gain, 0.0)
            first_pass = jnp.sum(root * pull, axis=1, keepdims=True)
            shift = jnp.sum(root * first_pass, axis=0, keepdims=True)
            weights_now[group * 2 * PAIRS + i] = member_root * root + shift

    flat_lines = lines.reshape(PARTS, 2, MEMBERS * 8, 128)

    def out_copy(part, j):
        return pltpu.make_async_copy(
            lines.at[part, j],
            analysis.at[:, pl.ds(pl.multiple_of(part * 8, 8), 8), pl.ds(j * 128, 128)],
            out_sem.at[part, j],
        )

    own.wait()

    @pl.loop(0, PARTS)
    def _(part):
        @pl.loop(1, PEERS)
        def _(i):
            block_copy(part, i).wait()

        @pl.loop(0, 2)
        def _(a):
            places = [part * 2 * SIDE + a * SIDE + b for b in range(SIDE)]
            fields = [gathered[place] for place in places]
            centres = [jnp.mean(field, axis=0, keepdims=True) for field in fields]
            updated = [
                product(weights_now[place], *split(field - centre)) + centre
                for place, field, centre in zip(places, fields, centres)
            ]
            for j in range(2):
                for m in range(MEMBERS // 8):
                    rows = swap_groups(
                        [block[m * 8 : m * 8 + 8] for block in updated[4 * j : 4 * j + 4]]
                    )
                    for r in range(BR):
                        at = pl.ds(m * 64 + a * BR + r, 8, stride=8)
                        flat_lines[part, j, at, :] = rows[r]

        for j in range(2):
            out_copy(part, j).start()

    @pl.loop(0, PARTS)
    def _(part):
        for j in range(2):
            out_copy(part, j).wait()

    store_c.wait()


def assimilate(*arguments):
    field = (ROWS, COLS)
    f32 = jnp.float32
    anywhere = pl.BlockSpec(memory_space=pl.ANY)
    local = pl.BlockSpec(memory_space=pltpu.VMEM)
    halo = pltpu.VMEM((STEPS, TILES, OWN, 128), f32)
    dma = pltpu.SemaphoreType.DMA
    square = pltpu.VMEM((BLOCKS, MEMBERS, 128), f32)
    return pl.pallas_call(
        assimilate_kernel,
        out_shape=(
            jax.ShapeDtypeStruct((MEMBERS, ROWS, 2 * 128), f32),
            jax.ShapeDtypeStruct((OWN, ROWS, COLS), f32),
        ),
        in_specs=[anywhere] * 6 + [local] * 4 + [pl.BlockSpec(memory_space=pltpu.SMEM)],
        out_specs=[anywhere] * 2,
        scratch_shapes=[
            *[pltpu.VMEM((TILES + 2, OWN, PAD_ROWS, 128), f32)] * 2,
            *[pltpu.VMEM((OWN, ROWS, COLS), f32)] * 2,
            *[pltpu.VMEM(field, f32)] * 4,
            *[pltpu.VMEM((8, COLS), f32)] * 2,
            *[pltpu.VMEM(field, f32)] * 5,
            *[halo] * 4,
            pltpu.VMEM((PEERS, BLOCKS, OWN, 128), f32),
            pltpu.VMEM((SIDE, 128), jnp.int32),
            *[pltpu.VMEM((SIDE, 128), f32)] * 2,
            pltpu.VMEM((PEERS, SIDE, 128), jnp.int32),
            pltpu.VMEM((PEERS, SIDE, OWN, 128), f32),
            pltpu.VMEM((SIDE, MEMBERS, 128), f32),
            pltpu.VMEM((SIDE + 2, SIDE + 2, 2 * OBS_MAX, 128), f32),
            *[pltpu.VMEM((PAIRS, 2 * HALF, 128), f32)] * 2,
            *[pltpu.VMEM((PAIRS, HALF, 128), f32)] * 3,
            square, square,
            pltpu.VMEM((PARTS, 2, MEMBERS, 8, 128), f32),
            dma((5,)), dma((TILES,)), dma((2,)), dma((2,)),
            dma((STEPS, 2)), dma((STEPS, 2)), dma((PARTS, PEERS)), dma((PARTS, PEERS)),
            dma((2,)), dma,
            dma((PEERS,)), dma((PEERS,)), dma((PEERS,)), dma((PEERS,)), dma((4,)), dma((4,)),
            dma((PARTS, 2)),
        ],
        compiler_params=pltpu.CompilerParams(
            collective_id=0, has_side_effects=True, vmem_limit_bytes=62 << 20
        ),
        name="assimilate",
    )(*arguments)


def solution(mesh):
    placed = (
        P("mem", "slab", None),
        P("mem", "slab", None),
        P("slab", None),
        P("slab", None),
        P("slab", None),
        P("slab", None),
        P("slab", "mem", None),
        P("slab", "mem", None),
        P("slab", "mem", None),
        P("slab", "mem"),
        P("slab", "mem", None),
    )
    return jax.shard_map(
        assimilate,
        mesh=mesh,
        in_specs=placed,
        out_specs=(P(None, "slab", "mem"), P("mem", "slab", None)),
        check_vma=False,
    )
```

```python
import math

import jax
import jax.numpy as jnp
from jax import lax
from jax.experimental import pallas as pl
from jax.experimental.pallas import tpu as pltpu
from jax.sharding import PartitionSpec as P

MEMBERS = 128
STEPS = 4
BR = 4
BC = 32
OBS_MAX = 16
NBR = 4
NS_ITERS = 7

PEERS = 16
SLABS = 8
OWN = 8
ROWS = 32
COLS = 4096
TILES = 32
PAD_ROWS = 48
BLOCKS = 64
SIDE = 8
PAIRS = 8
PARTS = 4
HALF = NBR * OBS_MAX

inflation = 1.1
ridge = (MEMBERS - 1) / inflation
member_root = math.sqrt(MEMBERS - 1)
side_weight = math.exp(-0.25)
corner_weight = math.exp(-0.5)
mesh_ids = pl.DeviceIdType.MESH

ways = (
    (2, 2), (0, 1), (1, 0), (1, 1), (3, 3), (0, 3), (3, 0), (1, 3), (3, 1), (0, 2), (2, 0),
    (2, 1), (1, 2), (2, 3), (3, 2),
)


def split(value):
    head = value.astype(jnp.bfloat16)
    return head, (value - head.astype(jnp.float32)).astype(jnp.bfloat16)


def product(left, head, tail):
    left_head, left_tail = split(left)
    both = jnp.concatenate([head, tail], axis=1)
    result = jnp.dot(
        jnp.concatenate([left_head, left_tail], axis=1),
        jnp.concatenate([both, both], axis=0),
        preferred_element_type=jnp.float32,
    )
    columns = head.shape[1]
    return result[:, :columns] + result[:, columns:]


def pair_product(left, right):
    same = (lax.broadcasted_iota(jnp.int32, (128, 128), 0) < HALF) == (
        lax.broadcasted_iota(jnp.int32, (128, 128), 1) < HALF
    )
    head, tail = (
        jnp.where(same, jnp.concatenate([part, part], axis=0), jnp.zeros((128, 128), jnp.bfloat16))
        for part in split(right)
    )
    return product(left, head, tail)


def swap_groups(rows):
    group = lax.broadcasted_iota(jnp.int32, (8, 128), 1) // BC
    even = group % 2 == 0
    low = group < 2
    near = [None] * 4
    for i in (0, 2):
        near[i] = jnp.where(even, rows[i], pltpu.roll(rows[i + 1], BC, 1))
        near[i + 1] = jnp.where(even, pltpu.roll(rows[i], 128 - BC, 1), rows[i + 1])
    out = [None] * 4
    for i in (0, 1):
        out[i] = jnp.where(low, near[i], pltpu.roll(near[i + 2], 64, 1))
        out[i + 2] = jnp.where(low, pltpu.roll(near[i], 64, 1), near[i + 2])
    return out


def assimilate_kernel(
    p_in, c_in, d_in, lp_in, lv_in, rate_in, cell_in, value_in, error_in, count_in, neighbour,
    analysis, c_out,
    p, p_other, c, c_other, lp, lv, rate, dif, dif_top, dif_low, keep, k_up, k_down, k_left, k_right,
    out_up, out_down, in_top, in_low, send,
    cells, values, roots, all_cells, obs_send, obs_in, obs_pad,
    rows_z, innov_z, now_x, now_m, now_d, weights_now, gathered, lines,
    load_sem, p_sem, dif_send, dif_recv, halo_send, halo_recv, send_sem, recv_sem, own_sem, c_sem,
    cell_send, cell_recv, obs_send_sem, obs_recv_sem, side_send, side_recv, out_sem,
):
    mem = lax.axis_index("mem")
    slab = lax.axis_index("slab")
    above = lax.rem(slab + SLABS - 1, SLABS)
    below = lax.rem(slab + 1, SLABS)

    def load_p(tile):
        return pltpu.make_async_copy(
            p_in.at[:, :, pl.ds(pl.multiple_of(tile * 128, 128), 128)],
            p.at[tile + 1, :, pl.ds(8, ROWS), :],
            p_sem.at[tile],
        )

    loads = [
        pltpu.make_async_copy(src, dst, load_sem.at[i])
        for i, (src, dst) in enumerate(
            ((d_in, dif), (lp_in, lp), (lv_in, lv), (rate_in, rate), (c_in, c))
        )
    ]
    for load in loads[:1]:
        load.start()

    @pl.loop(0, TILES)
    def _(tile):
        load_p(tile).start()

    for load in loads[1:]:
        load.start()

    lane = lax.broadcasted_iota(jnp.int32, (8, 128), 1)
    line = lax.broadcasted_iota(jnp.int32, (8, 128), 0)
    slot_group = lane // OBS_MAX

    def lay_out(piece_of):
        out = piece_of(0)
        for b in range(1, SIDE):
            out = jnp.where(slot_group == b, piece_of(b), out)
        return out

    def slots_of(ref):
        return lay_out(lambda b: jnp.concatenate([ref[:, b, :]] * SIDE, axis=1))

    cells[...] = slots_of(cell_in)
    values[...] = slots_of(value_in)
    counts = lay_out(lambda b: jnp.broadcast_to(count_in[:, b : b + 1], (SIDE, 128)))
    live = lax.rem(lane, OBS_MAX) < counts
    roots[...] = jnp.where(live, jnp.sqrt(slots_of(error_in)), 0.0)

    barrier = pltpu.get_barrier_semaphore()

    @pl.loop(1, PEERS)
    def _(i):
        pl.semaphore_signal(
            barrier, inc=1, device_id=(lax.rem(mem + i, PEERS), slab),
            device_id_type=pl.DeviceIdType.MESH,
        )

    for other in (above, below):
        pl.semaphore_signal(
            barrier, inc=1, device_id=(mem, other), device_id_type=pl.DeviceIdType.MESH
        )

    zero = jnp.zeros((8, 128), jnp.float32)
    for field in (p, p_other):
        for tile in (0, TILES + 1):
            for m in range(OWN):
                for i in range(PAD_ROWS // 8):
                    field[tile, m, i * 8 : i * 8 + 8, :] = zero

    pl.semaphore_wait(barrier, PEERS + 1)

    def dif_copy(i, src, dst, other):
        return pltpu.make_async_remote_copy(
            src_ref=src, dst_ref=dst, send_sem=dif_send.at[i], recv_sem=dif_recv.at[i],
            device_id=(mem, other), device_id_type=pl.DeviceIdType.MESH,
        )

    def cell_copy(i):
        return pltpu.make_async_remote_copy(
            src_ref=cells, dst_ref=all_cells.at[mem],
            send_sem=cell_send.at[i], recv_sem=cell_recv.at[i],
            device_id=(lax.rem(mem + i, PEERS), slab), device_id_type=mesh_ids,
        )

    @pl.loop(1, PEERS)
    def _(i):
        cell_copy(i).start()

    all_cells[mem] = cells[...]

    dif_copies = [
        dif_copy(0, d_in.at[pl.ds(24, 8)], dif_top, below),
        dif_copy(1, d_in.at[pl.ds(0, 8)], dif_low, above),
    ]
    for copy in dif_copies:
        copy.start()

    def halo_copy(step, i):
        src, dst, other = ((out_down, in_top, below), (out_up, in_low, above))[i]
        return pltpu.make_async_remote_copy(
            src_ref=src.at[step], dst_ref=dst.at[step],
            send_sem=halo_send.at[step, i], recv_sem=halo_recv.at[step, i],
            device_id=(mem, other), device_id_type=pl.DeviceIdType.MESH,
        )

    flat, flat_other = (
        field.reshape(TILES + 2, OWN * PAD_ROWS, 128) for field in (p, p_other)
    )

    def send_halo(step):
        for i in range(2):
            halo_copy(step, i).start()

    first_row = pl.ds(8, OWN, stride=PAD_ROWS)
    last_row = pl.ds(7 + ROWS, OWN, stride=PAD_ROWS)

    def clear_outside(field, tile):
        field[tile + 1, pl.ds(7, OWN, stride=PAD_ROWS), :] = zero
        field[tile + 1, pl.ds(8 + ROWS, OWN, stride=PAD_ROWS), :] = zero

    @pl.loop(0, TILES, unroll=8)
    def _(tile):
        clear_outside(flat_other, tile)

    @pl.loop(0, TILES)
    def _(tile):
        load_p(tile).wait()

    @pl.loop(0, TILES, unroll=8)
    def _(tile):
        clear_outside(flat, tile)
        out_up[0, tile] = flat[tile + 1, first_row, :]
        out_down[0, tile] = flat[tile + 1, last_row, :]

    send_halo(0)

    for load in loads:
        load.wait()
    for copy in dif_copies:
        copy.wait()

    first, last = lane == 0, lane == 127
    at_top, at_low = slab == 0, slab == SLABS - 1

    @pl.loop(0, TILES, unroll=4)
    def _(tile):
        here = pl.ds(pl.multiple_of(tile * 128, 128), 128)
        left = pl.ds(pl.multiple_of(jnp.maximum(tile - 1, 0) * 128, 128), 128)
        right = pl.ds(pl.multiple_of(jnp.minimum(tile + 1, TILES - 1) * 128, 128), 128)
        top_row = jnp.where(at_top, 0.0, dif_top[:, here])
        low_row = jnp.where(at_low, 0.0, dif_low[:, here])
        mids = [dif[i * 8 : i * 8 + 8, here] for i in range(4)]
        column = [top_row, *mids, low_row]
        for i in range(4):
            rows = slice(i * 8, i * 8 + 8)
            mid = mids[i]
            up = jnp.where(line == 0, pltpu.roll(column[i], 1, 0), pltpu.roll(mid, 1, 0))
            down = jnp.where(line == 7, pltpu.roll(column[i + 2], 7, 0), pltpu.roll(mid, 7, 0))
            next_left = jnp.where(tile == 0, 0.0, dif[rows, left])
            next_right = jnp.where(tile == TILES - 1, 0.0, dif[rows, right])
            west = jnp.where(first, pltpu.roll(next_left, 1, 1), pltpu.roll(mid, 1, 1))
            east = jnp.where(last, pltpu.roll(next_right, 127, 1), pltpu.roll(mid, 127, 1))
            sides = [0.1 * (mid + side) for side in (up, down, west, east)]
            for ref, side in zip((k_up, k_down, k_left, k_right), sides):
                ref[rows, here] = side
            keep[rows, here] = 1.0 - ((sides[0] + sides[1]) + (sides[2] + sides[3]))
            lv[rows, here] = lv[rows, here] * rate[rows, here]

    wide = 4

    def advance(now, content_now, later, content_later):

        @pl.loop(0, TILES // wide)
        def _(group):
            for row_tile in range(ROWS // 8):
                rows = slice(row_tile * 8, row_tile * 8 + 8)
                base = 8 + row_tile * 8
                heres = [
                    pl.ds(pl.multiple_of((group * wide + j) * 128, 128), 128) for j in range(wide)
                ]
                weights = [
                    [ref[rows, here] for ref in (keep, k_up, k_down, k_left, k_right, lp, lv, rate)]
                    for here in heres
                ]
                for m in range(OWN):
                    mids = [
                        now[group * wide + j, m, base : base + 8, :] for j in range(wide + 2)
                    ]
                    to_right = [pltpu.roll(mids[j], 1, 1) for j in range(wide + 1)]
                    to_left = [None] + [pltpu.roll(mids[j], 127, 1) for j in range(1, wide + 2)]
                    for j in range(wide):
                        keep_w, up_w, down_w, left_w, right_w, lp_w, lv_w, rate_w = weights[j]
                        tile = group * wide + j + 1
                        mid = mids[j + 1]
                        up = now[tile, m, base - 1 : base + 7, :]
                        down = now[tile, m, base + 1 : base + 9, :]
                        west = jnp.where(first, to_right[j], to_right[j + 1])
                        east = jnp.where(last, to_left[j + 2], to_left[j + 1])
                        content = content_now[m, rows, heres[j]]
                        inverse = pltpu.reciprocal(lp_w + jnp.abs(mid), approx=True)
                        release = rate_w * content - (lv_w * mid) * inverse
                        flow = (up_w * up + down_w * down) + (left_w * west + right_w * east)
                        later[tile, m, base : base + 8, :] = (
                            keep_w * mid + flow + release
                        )
                        content_later[m, rows, heres[j]] = content - release

    def one_step(step, now, content_now, later, content_later, flat_later, more):
        advance(now, content_now, later, content_later)
        for i in range(2):
            halo_copy(step, i).wait()
        following = lax.rem(step + 1, STEPS)

        @pl.loop(0, TILES, unroll=8)
        def _(tile):
            here = pl.ds(pl.multiple_of(tile * 128, 128), 128)
            top = jnp.where(at_top, 0.0, in_top[step, tile]) * k_up[0:1, here]
            low = jnp.where(at_low, 0.0, in_low[step, tile]) * k_down[ROWS - 1 : ROWS, here]
            top = flat_later[tile + 1, first_row, :] + top
            low = flat_later[tile + 1, last_row, :] + low
            flat_later[tile + 1, first_row, :] = top
            flat_later[tile + 1, last_row, :] = low
            out_up[following, tile] = top
            out_down[following, tile] = low

        @pl.when(more)
        def _():
            send_halo(step + 1)

    @pl.loop(0, STEPS // 2)
    def _(pair):
        one_step(2 * pair, p, c, p_other, c_other, flat_other, True)
        one_step(2 * pair + 1, p_other, c_other, p, c, flat, pair < STEPS // 2 - 1)

    store_c = pltpu.make_async_copy(c, c_out, c_sem)
    store_c.start()

    @pl.loop(1, PEERS)
    def _(i):
        cell_copy(i).wait()

    def to_blocks(target):
        for a in range(SIDE):
            index = jnp.broadcast_to(all_cells[target, a : a + 1, :], (OWN, 128))
            observed = jnp.zeros((OWN, 128), jnp.float32)
            for j in range(2):
                lines = [
                    flat[target * 2 + j + 1, pl.ds(8 + a * BR + r, OWN, stride=PAD_ROWS), :]
                    for r in range(BR)
                ]
                blocks = swap_groups(lines)
                for b in range(4):
                    send[target, a * SIDE + j * 4 + b] = blocks[b]
                    picked = jnp.take_along_axis(blocks[b], index, axis=1)
                    observed = jnp.where(slot_group == j * 4 + b, picked, observed)
            obs_send[target, a] = observed

    mine = pl.ds(pl.multiple_of(mem * OWN, OWN), OWN)

    def place_of(code):
        return lax.rem(mem // 4 + code // 4, 4) * 4 + lax.rem(mem + code, 4)

    def obs_copy(i):
        target = place_of(i)
        return pltpu.make_async_remote_copy(
            src_ref=obs_send.at[target], dst_ref=obs_in.at[:, mine, :],
            send_sem=obs_send_sem.at[i], recv_sem=obs_recv_sem.at[i],
            device_id=(target, slab), device_id_type=mesh_ids,
        )

    def block_copy(part, i):
        target = place_of(i)
        blocks = pl.ds(part * 2 * SIDE, 2 * SIDE)
        return pltpu.make_async_remote_copy(
            src_ref=send.at[target, blocks], dst_ref=gathered.at[blocks, mine, :],
            send_sem=send_sem.at[part, i], recv_sem=recv_sem.at[part, i],
            device_id=(target, slab), device_id_type=mesh_ids,
        )

    @pl.loop(1, PEERS)
    def _(i):
        code = lax.rem(7 * i, PEERS)
        to_blocks(place_of(code))
        obs_copy(code).start()
        block_copy(0, code).start()

    to_blocks(mem)
    own = pltpu.make_async_copy(send.at[mem], gathered.at[:, mine, :], own_sem.at[0])
    own.start()
    own_obs = pltpu.make_async_copy(obs_send.at[mem], obs_in.at[:, mine, :], own_sem.at[1])
    own_obs.start()
    own_obs.wait()

    @pl.loop(1, PEERS)
    def _(i):
        obs_copy(i).wait()

    @pl.loop(0, SIDE)
    def _(a):
        seen = obs_in[a]
        centre = jnp.mean(seen, axis=0, keepdims=True)
        root = roots[pl.ds(a, 1), :]
        spread = ((seen - centre) * root).T
        innovation = jnp.broadcast_to((values[pl.ds(a, 1), :] - centre) * root, (128, 128)).T
        for b in range(SIDE):
            obs_pad[a + 1, b + 1, 0:OBS_MAX, :] = spread[b * OBS_MAX : (b + 1) * OBS_MAX]
            obs_pad[a + 1, b + 1, OBS_MAX:, :] = innovation[b * OBS_MAX : (b + 1) * OBS_MAX]

    def side_copy(i):
        src, dst, device = (
            (obs_pad.at[1:9, 8], obs_pad.at[1:9, 0], (lax.rem(mem + 1, PEERS), slab)),
            (obs_pad.at[1:9, 1], obs_pad.at[1:9, 9], (lax.rem(mem + PEERS - 1, PEERS), slab)),
            (obs_pad.at[8], obs_pad.at[0], (mem, below)),
            (obs_pad.at[1], obs_pad.at[9], (mem, above)),
        )[i]
        return pltpu.make_async_remote_copy(
            src_ref=src, dst_ref=dst, send_sem=side_send.at[i], recv_sem=side_recv.at[i],
            device_id=device, device_id_type=mesh_ids,
        )

    blank = jnp.zeros((2 * OBS_MAX, 128), jnp.float32)
    for sides, conditions in (
        ((0, 1), (mem == 0, mem == PEERS - 1)),
        ((2, 3), (at_top, at_low)),
    ):
        for i in sides:
            side_copy(i).start()
        for i in sides:
            side_copy(i).wait()
        if sides[0] == 0:

            @pl.loop(1, PARTS)
            def _(part):
                for way in ways:
                    block_copy(part, 4 * way[0] + way[1]).start()

        for i, condition in zip(sides, conditions):

            @pl.when(condition)
            def _(i=i):
                @pl.loop(*((1, SIDE + 1) if i < 2 else (0, SIDE + 2)))
                def _(place):
                    if i < 2:
                        obs_pad[place, 0 if i == 0 else SIDE + 1] = blank
                    else:
                        obs_pad[0 if i == 2 else SIDE + 1, place] = blank

    half_lane = lax.broadcasted_iota(jnp.int32, (1, 128), 1) < HALF
    diagonal = lax.broadcasted_iota(jnp.int32, (HALF, 128), 0) == lax.rem(
        lax.broadcasted_iota(jnp.int32, (HALF, 128), 1), HALF
    )
    pair_eye = jnp.where(diagonal, 1.0, 0.0)
    eye = lax.broadcasted_iota(jnp.int32, (128, 128), 0) == lax.broadcasted_iota(
        jnp.int32, (128, 128), 1
    )
    no_rows = jnp.zeros((HALF, 128), jnp.float32)

    @pl.loop(0, BLOCKS // (2 * PAIRS))
    def _(group):
        start = []
        for pair in range(PAIRS):
            for i in range(2 * NBR):
                place = 2 * pair + i // NBR
                a = group * (PAIRS // 4) + place // SIDE
                b = place % SIDE
                code = neighbour[a, i % NBR, b]
                down_by = lax.div(code, 3)
                right_by = code - 3 * down_by
                block = obs_pad[a + down_by, b + right_by]
                far = (down_by != 1).astype(jnp.int32) + (right_by != 1).astype(jnp.int32)
                weight = jnp.where(
                    far == 0, 1.0, jnp.where(far == 1, side_weight, corner_weight)
                )
                rows_z[pair, i * OBS_MAX : (i + 1) * OBS_MAX, :] = weight * block[:OBS_MAX]
                innov_z[pair, i * OBS_MAX : (i + 1) * OBS_MAX, :] = weight * block[OBS_MAX:]
        rows = [rows_z[pair] for pair in range(PAIRS)]
        grams = [product(z, *split(z.T)) for z in rows]
        smalls = [jnp.where(half_lane, gram[:HALF], gram[HALF:]) for gram in grams]
        traces = [
            jnp.sum(jnp.where(diagonal, small, 0.0), axis=0, keepdims=True) for small in smalls
        ]
        totals = [
            [
                MEMBERS * ridge + jnp.sum(jnp.where(side, trace, 0.0), axis=1, keepdims=True)
                for side in (half_lane, jnp.logical_not(half_lane))
            ]
            for trace in traces
        ]
        for pair, (small, total) in enumerate(zip(smalls, totals)):
            scale = 1.0 / jnp.where(half_lane, total[0], total[1])
            low = ridge * scale
            now_x[pair] = small * scale + low * pair_eye
            now_m[pair] = no_rows
            now_d[pair] = pair_eye
            start.append((low, jnp.ones_like(low)))

        def sweep(_, carry):
            states = [(now_x[i], now_m[i], now_d[i]) for i in range(PAIRS)]
            by_x = [
                pair_product(jnp.concatenate(state, axis=0), state[0]) for state in states
            ]
            factors = [
                0.25 * result[:HALF] - 1.5 * state[0] + 2.25 * pair_eye
                for result, state in zip(by_x, states)
            ]
            by_f = [
                pair_product(jnp.concatenate([x, d], axis=0), factor)
                for (x, _, d), factor in zip(states, factors)
            ]
            ahead = []
            later = []
            for (x, m, d), (low, gain), first, second in zip(states, carry, by_x, by_f):
                new_d = (
                    second[HALF:]
                    + (0.25 * low) * first[2 * HALF :]
                    + (0.25 * low * (low - 6.0)) * d
                )
                new_m = 1.5 * m - 0.5 * first[HALF : 2 * HALF] - (0.5 * gain) * d
                later.append((second[:HALF], new_m, new_d))
                shrink = 1.5 - 0.5 * low
                ahead.append((low * shrink * shrink, gain * shrink))
            for i in range(PAIRS):
                now_x[i], now_m[i], now_d[i] = later[i]
            return tuple(ahead)

        last_low = lax.fori_loop(0, NS_ITERS - 1, sweep, tuple(start))
        states = [(now_x[i], now_m[i], now_d[i]) for i in range(PAIRS)]
        rows = [rows_z[pair] for pair in range(PAIRS)]
        by_x = [pair_product(m, x) for x, m, _ in states]
        ends = []
        for (_, m, d), (_, gain), total, result in zip(states, last_low, totals, by_x):
            both = jnp.where(half_lane, total[0], total[1])
            m = 1.5 * m - 0.5 * result - (0.5 * gain) * d
            m = m * (1.0 / (both * jnp.sqrt(both)))
            ends.append(
                jnp.concatenate(
                    [jnp.where(half_lane, m, 0.0), jnp.where(half_lane, 0.0, m)], axis=0
                )
            )
        by_z = [product(end, *split(z)) for end, z in zip(ends, rows)]
        wide_z = [
            jnp.concatenate(
                [
                    jnp.concatenate([m_z[:HALF], no_rows], axis=0),
                    jnp.concatenate([no_rows, m_z[HALF:]], axis=0),
                ],
                axis=1,
            )
            for m_z in by_z
        ]
        roots_both = [product(z.T, *split(right)) for z, right in zip(rows, wide_z)]
        gains = []
        pulls = []
        for pair, (z, total) in enumerate(zip(rows, totals)):
            for side in range(2):
                low = ridge / total[side]
                gain = 1.0 / jnp.sqrt(total[side])
                for _ in range(NS_ITERS):
                    shrink = 1.5 - 0.5 * low
                    low, gain = low * shrink * shrink, gain * shrink
                gains.append(gain)
                own_rows = slice(side * HALF, side * HALF + HALF)
                pulls.append(
                    jnp.sum(innov_z[pair, own_rows] * z[own_rows], axis=0, keepdims=True)
                )
        for i, (gain, pull) in enumerate(zip(gains, pulls)):
            column = i % 2 * 128
            root = roots_both[i // 2][:, column : column + 128] + jnp.where(eye, gain, 0.0)
            first_pass = jnp.sum(root * pull, axis=1, keepdims=True)
            shift = jnp.sum(root * first_pass, axis=0, keepdims=True)
            weights_now[group * 2 * PAIRS + i] = member_root * root + shift

    flat_lines = lines.reshape(PARTS, 2, MEMBERS * 8, 128)

    def out_copy(part, j):
        return pltpu.make_async_copy(
            lines.at[part, j],
            analysis.at[:, pl.ds(pl.multiple_of(part * 8, 8), 8), pl.ds(j * 128, 128)],
            out_sem.at[part, j],
        )

    own.wait()

    @pl.loop(0, PARTS)
    def _(part):
        @pl.loop(1, PEERS)
        def _(i):
            block_copy(part, i).wait()

        @pl.loop(0, 2)
        def _(a):
            places = [part * 2 * SIDE + a * SIDE + b for b in range(SIDE)]
            fields = [gathered[place] for place in places]
            centres = [jnp.mean(field, axis=0, keepdims=True) for field in fields]
            updated = [
                product(weights_now[place], *split(field - centre)) + centre
                for place, field, centre in zip(places, fields, centres)
            ]
            for j in range(2):
                for m in range(MEMBERS // 8):
                    rows = swap_groups(
                        [block[m * 8 : m * 8 + 8] for block in updated[4 * j : 4 * j + 4]]
                    )
                    for r in range(BR):
                        at = pl.ds(m * 64 + a * BR + r, 8, stride=8)
                        flat_lines[part, j, at, :] = rows[r]

        for j in range(2):
            out_copy(part, j).start()

    @pl.loop(0, PARTS)
    def _(part):
        for j in range(2):
            out_copy(part, j).wait()

    store_c.wait()


def assimilate(*arguments):
    field = (ROWS, COLS)
    f32 = jnp.float32
    anywhere = pl.BlockSpec(memory_space=pl.ANY)
    local = pl.BlockSpec(memory_space=pltpu.VMEM)
    halo = pltpu.VMEM((STEPS, TILES, OWN, 128), f32)
    dma = pltpu.SemaphoreType.DMA
    square = pltpu.VMEM((BLOCKS, MEMBERS, 128), f32)
    return pl.pallas_call(
        assimilate_kernel,
        out_shape=(
            jax.ShapeDtypeStruct((MEMBERS, ROWS, 2 * 128), f32),
            jax.ShapeDtypeStruct((OWN, ROWS, COLS), f32),
        ),
        in_specs=[anywhere] * 6 + [local] * 4 + [pl.BlockSpec(memory_space=pltpu.SMEM)],
        out_specs=[anywhere] * 2,
        scratch_shapes=[
            *[pltpu.VMEM((TILES + 2, OWN, PAD_ROWS, 128), f32)] * 2,
            *[pltpu.VMEM((OWN, ROWS, COLS), f32)] * 2,
            *[pltpu.VMEM(field, f32)] * 4,
            *[pltpu.VMEM((8, COLS), f32)] * 2,
            *[pltpu.VMEM(field, f32)] * 5,
            *[halo] * 4,
            pltpu.VMEM((PEERS, BLOCKS, OWN, 128), f32),
            pltpu.VMEM((SIDE, 128), jnp.int32),
            *[pltpu.VMEM((SIDE, 128), f32)] * 2,
            pltpu.VMEM((PEERS, SIDE, 128), jnp.int32),
            pltpu.VMEM((PEERS, SIDE, OWN, 128), f32),
            pltpu.VMEM((SIDE, MEMBERS, 128), f32),
            pltpu.VMEM((SIDE + 2, SIDE + 2, 2 * OBS_MAX, 128), f32),
            *[pltpu.VMEM((PAIRS, 2 * HALF, 128), f32)] * 2,
            *[pltpu.VMEM((PAIRS, HALF, 128), f32)] * 3,
            square, square,
            pltpu.VMEM((PARTS, 2, MEMBERS, 8, 128), f32),
            dma((5,)), dma((TILES,)), dma((2,)), dma((2,)),
            dma((STEPS, 2)), dma((STEPS, 2)), dma((PARTS, PEERS)), dma((PARTS, PEERS)),
            dma((2,)), dma,
            dma((PEERS,)), dma((PEERS,)), dma((PEERS,)), dma((PEERS,)), dma((4,)), dma((4,)),
            dma((PARTS, 2)),
        ],
        compiler_params=pltpu.CompilerParams(
            collective_id=0, has_side_effects=True, vmem_limit_bytes=62 << 20
        ),
        name="assimilate",
    )(*arguments)


def on_device(*arguments):
    return assimilate(*arguments[:-1], arguments[-1].transpose(0, 2, 1))


def solution(mesh):
    placed = (
        P("mem", "slab", None),
        P("mem", "slab", None),
        P("slab", None),
        P("slab", None),
        P("slab", None),
        P("slab", None),
        P("slab", "mem", None),
        P("slab", "mem", None),
        P("slab", "mem", None),
        P("slab", "mem"),
        P("slab", "mem", None),
    )
    return jax.shard_map(
        on_device,
        mesh=mesh,
        in_specs=placed,
        out_specs=(P(None, "slab", "mem"), P("mem", "slab", None)),
        check_vma=False,
    )
```

```python
import math

import jax
import jax.numpy as jnp
from jax import lax
from jax.experimental import pallas as pl
from jax.experimental.pallas import tpu as pltpu
from jax.sharding import PartitionSpec as P

MEMBERS = 128
STEPS = 4
BR = 4
BC = 32
OBS_MAX = 16
NBR = 4
NS_ITERS = 7

PEERS = 16
SLABS = 8
OWN = 8
ROWS = 32
COLS = 4096
TILES = 32
PAD_ROWS = 48
BLOCKS = 64
SIDE = 8
PAIRS = 8
PARTS = 4
HALF = NBR * OBS_MAX

inflation = 1.1
ridge = (MEMBERS - 1) / inflation
member_root = math.sqrt(MEMBERS - 1)
side_weight = math.exp(-0.25)
corner_weight = math.exp(-0.5)
mesh_ids = pl.DeviceIdType.MESH

ways = (
    (2, 2), (0, 1), (1, 0), (1, 1), (3, 3), (0, 3), (3, 0), (1, 3), (3, 1), (0, 2), (2, 0),
    (2, 1), (1, 2), (2, 3), (3, 2),
)


def split(value):
    head = value.astype(jnp.bfloat16)
    return head, (value - head.astype(jnp.float32)).astype(jnp.bfloat16)


def product(left, head, tail):
    left_head, left_tail = split(left)
    both = jnp.concatenate([head, tail], axis=1)
    result = jnp.dot(
        jnp.concatenate([left_head, left_tail], axis=1),
        jnp.concatenate([both, both], axis=0),
        preferred_element_type=jnp.float32,
    )
    columns = head.shape[1]
    return result[:, :columns] + result[:, columns:]


def pair_product(left, right):
    same = (lax.broadcasted_iota(jnp.int32, (128, 128), 0) < HALF) == (
        lax.broadcasted_iota(jnp.int32, (128, 128), 1) < HALF
    )
    head, tail = (
        jnp.where(same, jnp.concatenate([part, part], axis=0), jnp.zeros((128, 128), jnp.bfloat16))
        for part in split(right)
    )
    return product(left, head, tail)


def swap_groups(rows):
    group = lax.broadcasted_iota(jnp.int32, (8, 128), 1) // BC
    even = group % 2 == 0
    low = group < 2
    near = [None] * 4
    for i in (0, 2):
        near[i] = jnp.where(even, rows[i], pltpu.roll(rows[i + 1], BC, 1))
        near[i + 1] = jnp.where(even, pltpu.roll(rows[i], 128 - BC, 1), rows[i + 1])
    out = [None] * 4
    for i in (0, 1):
        out[i] = jnp.where(low, near[i], pltpu.roll(near[i + 2], 64, 1))
        out[i + 2] = jnp.where(low, pltpu.roll(near[i], 64, 1), near[i + 2])
    return out


def assimilate_kernel(
    p_in, c_in, d_in, lp_in, lv_in, rate_in, cell_in, value_in, error_in, count_in, neighbour,
    analysis, c_out,
    p, p_other, c, c_other, lp, lv, rate, dif, dif_top, dif_low, keep, k_up, k_down, k_left, k_right,
    out_up, out_down, in_top, in_low, send,
    cells, values, roots, all_cells, obs_send, obs_in, obs_pad,
    rows_z, innov_z, now_x, now_m, now_d, weights_now, gathered, lines,
    load_sem, p_sem, dif_send, dif_recv, halo_send, halo_recv, send_sem, recv_sem, own_sem, c_sem,
    cell_send, cell_recv, obs_send_sem, obs_recv_sem, side_send, side_recv, out_sem,
):
    mem = lax.axis_index("mem")
    slab = lax.axis_index("slab")
    above = lax.rem(slab + SLABS - 1, SLABS)
    below = lax.rem(slab + 1, SLABS)

    def load_p(tile):
        return pltpu.make_async_copy(
            p_in.at[:, :, pl.ds(pl.multiple_of(tile * 128, 128), 128)],
            p.at[tile + 1, :, pl.ds(8, ROWS), :],
            p_sem.at[tile],
        )

    loads = [
        pltpu.make_async_copy(src, dst, load_sem.at[i])
        for i, (src, dst) in enumerate(
            ((d_in, dif), (lp_in, lp), (lv_in, lv), (rate_in, rate), (c_in, c))
        )
    ]
    for load in loads[:1]:
        load.start()

    @pl.loop(0, TILES)
    def _(tile):
        load_p(tile).start()

    for load in loads[1:]:
        load.start()

    barrier = pltpu.get_barrier_semaphore()

    @pl.loop(1, PEERS)
    def _(i):
        pl.semaphore_signal(
            barrier, inc=1, device_id=(lax.rem(mem + i, PEERS), slab),
            device_id_type=pl.DeviceIdType.MESH,
        )

    for other in (above, below):
        pl.semaphore_signal(
            barrier, inc=1, device_id=(mem, other), device_id_type=pl.DeviceIdType.MESH
        )

    lane = lax.broadcasted_iota(jnp.int32, (8, 128), 1)
    line = lax.broadcasted_iota(jnp.int32, (8, 128), 0)
    slot_group = lane // OBS_MAX

    def lay_out(piece_of):
        out = piece_of(0)
        for b in range(1, SIDE):
            out = jnp.where(slot_group == b, piece_of(b), out)
        return out

    def slots_of(ref):
        return lay_out(lambda b: jnp.concatenate([ref[:, b, :]] * SIDE, axis=1))

    cells[...] = slots_of(cell_in)
    values[...] = slots_of(value_in)
    counts = lay_out(lambda b: jnp.broadcast_to(count_in[:, b : b + 1], (SIDE, 128)))
    live = lax.rem(lane, OBS_MAX) < counts
    roots[...] = jnp.where(live, jnp.sqrt(slots_of(error_in)), 0.0)

    zero = jnp.zeros((8, 128), jnp.float32)
    for field in (p, p_other):
        for tile in (0, TILES + 1):
            for m in range(OWN):
                for i in range(PAD_ROWS // 8):
                    field[tile, m, i * 8 : i * 8 + 8, :] = zero

    pl.semaphore_wait(barrier, PEERS + 1)

    def dif_copy(i, src, dst, other):
        return pltpu.make_async_remote_copy(
            src_ref=src, dst_ref=dst, send_sem=dif_send.at[i], recv_sem=dif_recv.at[i],
            device_id=(mem, other), device_id_type=pl.DeviceIdType.MESH,
        )

    def cell_copy(i):
        return pltpu.make_async_remote_copy(
            src_ref=cells, dst_ref=all_cells.at[mem],
            send_sem=cell_send.at[i], recv_sem=cell_recv.at[i],
            device_id=(lax.rem(mem + i, PEERS), slab), device_id_type=mesh_ids,
        )

    @pl.loop(1, PEERS)
    def _(i):
        cell_copy(i).start()

    all_cells[mem] = cells[...]

    dif_copies = [
        dif_copy(0, d_in.at[pl.ds(24, 8)], dif_top, below),
        dif_copy(1, d_in.at[pl.ds(0, 8)], dif_low, above),
    ]
    for copy in dif_copies:
        copy.start()

    def halo_copy(step, i):
        src, dst, other = ((out_down, in_top, below), (out_up, in_low, above))[i]
        return pltpu.make_async_remote_copy(
            src_ref=src.at[step], dst_ref=dst.at[step],
            send_sem=halo_send.at[step, i], recv_sem=halo_recv.at[step, i],
            device_id=(mem, other), device_id_type=pl.DeviceIdType.MESH,
        )

    flat, flat_other = (
        field.reshape(TILES + 2, OWN * PAD_ROWS, 128) for field in (p, p_other)
    )

    def send_halo(step):
        for i in range(2):
            halo_copy(step, i).start()

    first_row = pl.ds(8, OWN, stride=PAD_ROWS)
    last_row = pl.ds(7 + ROWS, OWN, stride=PAD_ROWS)

    def clear_outside(field, tile):
        field[tile + 1, pl.ds(7, OWN, stride=PAD_ROWS), :] = zero
        field[tile + 1, pl.ds(8 + ROWS, OWN, stride=PAD_ROWS), :] = zero

    @pl.loop(0, TILES, unroll=8)
    def _(tile):
        clear_outside(flat_other, tile)

    @pl.loop(0, TILES)
    def _(tile):
        load_p(tile).wait()

    @pl.loop(0, TILES, unroll=8)
    def _(tile):
        clear_outside(flat, tile)
        out_up[0, tile] = flat[tile + 1, first_row, :]
        out_down[0, tile] = flat[tile + 1, last_row, :]

    send_halo(0)

    for load in loads:
        load.wait()
    for copy in dif_copies:
        copy.wait()

    first, last = lane == 0, lane == 127
    at_top, at_low = slab == 0, slab == SLABS - 1

    @pl.loop(0, TILES, unroll=4)
    def _(tile):
        here = pl.ds(pl.multiple_of(tile * 128, 128), 128)
        left = pl.ds(pl.multiple_of(jnp.maximum(tile - 1, 0) * 128, 128), 128)
        right = pl.ds(pl.multiple_of(jnp.minimum(tile + 1, TILES - 1) * 128, 128), 128)
        top_row = jnp.where(at_top, 0.0, dif_top[:, here])
        low_row = jnp.where(at_low, 0.0, dif_low[:, here])
        mids = [dif[i * 8 : i * 8 + 8, here] for i in range(4)]
        column = [top_row, *mids, low_row]
        for i in range(4):
            rows = slice(i * 8, i * 8 + 8)
            mid = mids[i]
            up = jnp.where(line == 0, pltpu.roll(column[i], 1, 0), pltpu.roll(mid, 1, 0))
            down = jnp.where(line == 7, pltpu.roll(column[i + 2], 7, 0), pltpu.roll(mid, 7, 0))
            next_left = jnp.where(tile == 0, 0.0, dif[rows, left])
            next_right = jnp.where(tile == TILES - 1, 0.0, dif[rows, right])
            west = jnp.where(first, pltpu.roll(next_left, 1, 1), pltpu.roll(mid, 1, 1))
            east = jnp.where(last, pltpu.roll(next_right, 127, 1), pltpu.roll(mid, 127, 1))
            sides = [0.1 * (mid + side) for side in (up, down, west, east)]
            for ref, side in zip((k_up, k_down, k_left, k_right), sides):
                ref[rows, here] = side
            keep[rows, here] = 1.0 - ((sides[0] + sides[1]) + (sides[2] + sides[3]))
            lv[rows, here] = lv[rows, here] * rate[rows, here]

    wide = 4

    def advance(now, content_now, later, content_later):

        @pl.loop(0, TILES // wide)
        def _(group):
            for row_tile in range(ROWS // 8):
                rows = slice(row_tile * 8, row_tile * 8 + 8)
                base = 8 + row_tile * 8
                heres = [
                    pl.ds(pl.multiple_of((group * wide + j) * 128, 128), 128) for j in range(wide)
                ]
                weights = [
                    [ref[rows, here] for ref in (keep, k_up, k_down, k_left, k_right, lp, lv, rate)]
                    for here in heres
                ]
                for m in range(OWN):
                    mids = [
                        now[group * wide + j, m, base : base + 8, :] for j in range(wide + 2)
                    ]
                    to_right = [pltpu.roll(mids[j], 1, 1) for j in range(wide + 1)]
                    to_left = [None] + [pltpu.roll(mids[j], 127, 1) for j in range(1, wide + 2)]
                    for j in range(wide):
                        keep_w, up_w, down_w, left_w, right_w, lp_w, lv_w, rate_w = weights[j]
                        tile = group * wide + j + 1
                        mid = mids[j + 1]
                        up = now[tile, m, base - 1 : base + 7, :]
                        down = now[tile, m, base + 1 : base + 9, :]
                        west = jnp.where(first, to_right[j], to_right[j + 1])
                        east = jnp.where(last, to_left[j + 2], to_left[j + 1])
                        content = content_now[m, rows, heres[j]]
                        inverse = pltpu.reciprocal(lp_w + jnp.abs(mid), approx=True)
                        release = rate_w * content - (lv_w * mid) * inverse
                        flow = (up_w * up + down_w * down) + (left_w * west + right_w * east)
                        later[tile, m, base : base + 8, :] = (
                            keep_w * mid + flow + release
                        )
                        content_later[m, rows, heres[j]] = content - release

    def one_step(step, now, content_now, later, content_later, flat_later, more):
        advance(now, content_now, later, content_later)
        for i in range(2):
            halo_copy(step, i).wait()
        following = lax.rem(step + 1, STEPS)

        @pl.loop(0, TILES, unroll=8)
        def _(tile):
            here = pl.ds(pl.multiple_of(tile * 128, 128), 128)
            top = jnp.where(at_top, 0.0, in_top[step, tile]) * k_up[0:1, here]
            low = jnp.where(at_low, 0.0, in_low[step, tile]) * k_down[ROWS - 1 : ROWS, here]
            top = flat_later[tile + 1, first_row, :] + top
            low = flat_later[tile + 1, last_row, :] + low
            flat_later[tile + 1, first_row, :] = top
            flat_later[tile + 1, last_row, :] = low
            out_up[following, tile] = top
            out_down[following, tile] = low

        @pl.when(more)
        def _():
            send_halo(step + 1)

    @pl.loop(0, STEPS // 2)
    def _(pair):
        one_step(2 * pair, p, c, p_other, c_other, flat_other, True)
        one_step(2 * pair + 1, p_other, c_other, p, c, flat, pair < STEPS // 2 - 1)

    store_c = pltpu.make_async_copy(c, c_out, c_sem)
    store_c.start()

    @pl.loop(1, PEERS)
    def _(i):
        cell_copy(i).wait()

    def to_blocks(target):
        for a in range(SIDE):
            index = jnp.broadcast_to(all_cells[target, a : a + 1, :], (OWN, 128))
            observed = jnp.zeros((OWN, 128), jnp.float32)
            for j in range(2):
                lines = [
                    flat[target * 2 + j + 1, pl.ds(8 + a * BR + r, OWN, stride=PAD_ROWS), :]
                    for r in range(BR)
                ]
                blocks = swap_groups(lines)
                for b in range(4):
                    send[target, a * SIDE + j * 4 + b] = blocks[b]
                    picked = jnp.take_along_axis(blocks[b], index, axis=1)
                    observed = jnp.where(slot_group == j * 4 + b, picked, observed)
            obs_send[target, a] = observed

    mine = pl.ds(pl.multiple_of(mem * OWN, OWN), OWN)

    def place_of(code):
        return lax.rem(mem // 4 + code // 4, 4) * 4 + lax.rem(mem + code, 4)

    def obs_copy(i):
        target = place_of(i)
        return pltpu.make_async_remote_copy(
            src_ref=obs_send.at[target], dst_ref=obs_in.at[:, mine, :],
            send_sem=obs_send_sem.at[i], recv_sem=obs_recv_sem.at[i],
            device_id=(target, slab), device_id_type=mesh_ids,
        )

    def block_copy(part, i):
        target = place_of(i)
        blocks = pl.ds(part * 2 * SIDE, 2 * SIDE)
        return pltpu.make_async_remote_copy(
            src_ref=send.at[target, blocks], dst_ref=gathered.at[blocks, mine, :],
            send_sem=send_sem.at[part, i], recv_sem=recv_sem.at[part, i],
            device_id=(target, slab), device_id_type=mesh_ids,
        )

    @pl.loop(1, PEERS)
    def _(i):
        code = lax.rem(7 * i, PEERS)
        to_blocks(place_of(code))
        obs_copy(code).start()
        block_copy(0, code).start()

    to_blocks(mem)
    own = pltpu.make_async_copy(send.at[mem], gathered.at[:, mine, :], own_sem.at[0])
    own.start()
    own_obs = pltpu.make_async_copy(obs_send.at[mem], obs_in.at[:, mine, :], own_sem.at[1])
    own_obs.start()
    own_obs.wait()

    @pl.loop(1, PEERS)
    def _(i):
        obs_copy(i).wait()

    @pl.loop(0, SIDE)
    def _(a):
        seen = obs_in[a]
        centre = jnp.mean(seen, axis=0, keepdims=True)
        root = roots[pl.ds(a, 1), :]
        spread = ((seen - centre) * root).T
        innovation = jnp.broadcast_to((values[pl.ds(a, 1), :] - centre) * root, (128, 128)).T
        for b in range(SIDE):
            obs_pad[a + 1, b + 1, 0:OBS_MAX, :] = spread[b * OBS_MAX : (b + 1) * OBS_MAX]
            obs_pad[a + 1, b + 1, OBS_MAX:, :] = innovation[b * OBS_MAX : (b + 1) * OBS_MAX]

    def side_copy(i):
        src, dst, device = (
            (obs_pad.at[1:9, 8], obs_pad.at[1:9, 0], (lax.rem(mem + 1, PEERS), slab)),
            (obs_pad.at[1:9, 1], obs_pad.at[1:9, 9], (lax.rem(mem + PEERS - 1, PEERS), slab)),
            (obs_pad.at[8], obs_pad.at[0], (mem, below)),
            (obs_pad.at[1], obs_pad.at[9], (mem, above)),
        )[i]
        return pltpu.make_async_remote_copy(
            src_ref=src, dst_ref=dst, send_sem=side_send.at[i], recv_sem=side_recv.at[i],
            device_id=device, device_id_type=mesh_ids,
        )

    blank = jnp.zeros((2 * OBS_MAX, 128), jnp.float32)
    for sides, conditions in (
        ((0, 1), (mem == 0, mem == PEERS - 1)),
        ((2, 3), (at_top, at_low)),
    ):
        for i in sides:
            side_copy(i).start()
        for i in sides:
            side_copy(i).wait()
        if sides[0] == 0:

            @pl.loop(1, PARTS)
            def _(part):
                for way in ways:
                    block_copy(part, 4 * way[0] + way[1]).start()

        for i, condition in zip(sides, conditions):

            @pl.when(condition)
            def _(i=i):
                @pl.loop(*((1, SIDE + 1) if i < 2 else (0, SIDE + 2)))
                def _(place):
                    if i < 2:
                        obs_pad[place, 0 if i == 0 else SIDE + 1] = blank
                    else:
                        obs_pad[0 if i == 2 else SIDE + 1, place] = blank

    half_lane = lax.broadcasted_iota(jnp.int32, (1, 128), 1) < HALF
    diagonal = lax.broadcasted_iota(jnp.int32, (HALF, 128), 0) == lax.rem(
        lax.broadcasted_iota(jnp.int32, (HALF, 128), 1), HALF
    )
    pair_eye = jnp.where(diagonal, 1.0, 0.0)
    eye = lax.broadcasted_iota(jnp.int32, (128, 128), 0) == lax.broadcasted_iota(
        jnp.int32, (128, 128), 1
    )
    no_rows = jnp.zeros((HALF, 128), jnp.float32)

    @pl.loop(0, BLOCKS // (2 * PAIRS))
    def _(group):
        start = []
        for pair in range(PAIRS):
            for i in range(2 * NBR):
                place = 2 * pair + i // NBR
                a = group * (PAIRS // 4) + place // SIDE
                b = place % SIDE
                code = neighbour[a, i % NBR, b]
                down_by = lax.div(code, 3)
                right_by = code - 3 * down_by
                block = obs_pad[a + down_by, b + right_by]
                far = (down_by != 1).astype(jnp.int32) + (right_by != 1).astype(jnp.int32)
                weight = jnp.where(
                    far == 0, 1.0, jnp.where(far == 1, side_weight, corner_weight)
                )
                rows_z[pair, i * OBS_MAX : (i + 1) * OBS_MAX, :] = weight * block[:OBS_MAX]
                innov_z[pair, i * OBS_MAX : (i + 1) * OBS_MAX, :] = weight * block[OBS_MAX:]
        rows = [rows_z[pair] for pair in range(PAIRS)]
        grams = [product(z, *split(z.T)) for z in rows]
        smalls = [jnp.where(half_lane, gram[:HALF], gram[HALF:]) for gram in grams]
        traces = [
            jnp.sum(jnp.where(diagonal, small, 0.0), axis=0, keepdims=True) for small in smalls
        ]
        totals = [
            [
                MEMBERS * ridge + jnp.sum(jnp.where(side, trace, 0.0), axis=1, keepdims=True)
                for side in (half_lane, jnp.logical_not(half_lane))
            ]
            for trace in traces
        ]
        for pair, (small, total) in enumerate(zip(smalls, totals)):
            scale = 1.0 / jnp.where(half_lane, total[0], total[1])
            low = ridge * scale
            now_x[pair] = small * scale + low * pair_eye
            now_m[pair] = no_rows
            now_d[pair] = pair_eye
            start.append((low, jnp.ones_like(low)))

        def sweep(_, carry):
            states = [(now_x[i], now_m[i], now_d[i]) for i in range(PAIRS)]
            by_x = [
                pair_product(jnp.concatenate(state, axis=0), state[0]) for state in states
            ]
            factors = [
                0.25 * result[:HALF] - 1.5 * state[0] + 2.25 * pair_eye
                for result, state in zip(by_x, states)
            ]
            by_f = [
                pair_product(jnp.concatenate([x, d], axis=0), factor)
                for (x, _, d), factor in zip(states, factors)
            ]
            ahead = []
            later = []
            for (x, m, d), (low, gain), first, second in zip(states, carry, by_x, by_f):
                new_d = (
                    second[HALF:]
                    + (0.25 * low) * first[2 * HALF :]
                    + (0.25 * low * (low - 6.0)) * d
                )
                new_m = 1.5 * m - 0.5 * first[HALF : 2 * HALF] - (0.5 * gain) * d
                later.append((second[:HALF], new_m, new_d))
                shrink = 1.5 - 0.5 * low
                ahead.append((low * shrink * shrink, gain * shrink))
            for i in range(PAIRS):
                now_x[i], now_m[i], now_d[i] = later[i]
            return tuple(ahead)

        last_low = lax.fori_loop(0, NS_ITERS - 1, sweep, tuple(start))
        states = [(now_x[i], now_m[i], now_d[i]) for i in range(PAIRS)]
        rows = [rows_z[pair] for pair in range(PAIRS)]
        by_x = [pair_product(m, x) for x, m, _ in states]
        ends = []
        for (_, m, d), (_, gain), total, result in zip(states, last_low, totals, by_x):
            both = jnp.where(half_lane, total[0], total[1])
            m = 1.5 * m - 0.5 * result - (0.5 * gain) * d
            m = m * (1.0 / (both * jnp.sqrt(both)))
            ends.append(
                jnp.concatenate(
                    [jnp.where(half_lane, m, 0.0), jnp.where(half_lane, 0.0, m)], axis=0
                )
            )
        by_z = [product(end, *split(z)) for end, z in zip(ends, rows)]
        wide_z = [
            jnp.concatenate(
                [
                    jnp.concatenate([m_z[:HALF], no_rows], axis=0),
                    jnp.concatenate([no_rows, m_z[HALF:]], axis=0),
                ],
                axis=1,
            )
            for m_z in by_z
        ]
        roots_both = [product(z.T, *split(right)) for z, right in zip(rows, wide_z)]
        gains = []
        pulls = []
        for pair, (z, total) in enumerate(zip(rows, totals)):
            for side in range(2):
                low = ridge / total[side]
                gain = 1.0 / jnp.sqrt(total[side])
                for _ in range(NS_ITERS):
                    shrink = 1.5 - 0.5 * low
                    low, gain = low * shrink * shrink, gain * shrink
                gains.append(gain)
                own_rows = slice(side * HALF, side * HALF + HALF)
                pulls.append(
                    jnp.sum(innov_z[pair, own_rows] * z[own_rows], axis=0, keepdims=True)
                )
        for i, (gain, pull) in enumerate(zip(gains, pulls)):
            column = i % 2 * 128
            root = roots_both[i // 2][:, column : column + 128] + jnp.where(eye, gain, 0.0)
            first_pass = jnp.sum(root * pull, axis=1, keepdims=True)
            shift = jnp.sum(root * first_pass, axis=0, keepdims=True)
            weights_now[group * 2 * PAIRS + i] = member_root * root + shift

    flat_lines = lines.reshape(PARTS, 2, MEMBERS * 8, 128)

    def out_copy(part, j):
        return pltpu.make_async_copy(
            lines.at[part, j],
            analysis.at[:, pl.ds(pl.multiple_of(part * 8, 8), 8), pl.ds(j * 128, 128)],
            out_sem.at[part, j],
        )

    own.wait()

    @pl.loop(0, PARTS)
    def _(part):
        @pl.loop(1, PEERS)
        def _(i):
            block_copy(part, i).wait()

        @pl.loop(0, 2)
        def _(a):
            places = [part * 2 * SIDE + a * SIDE + b for b in range(SIDE)]
            fields = [gathered[place] for place in places]
            centres = [jnp.mean(field, axis=0, keepdims=True) for field in fields]
            updated = [
                product(weights_now[place], *split(field - centre)) + centre
                for place, field, centre in zip(places, fields, centres)
            ]
            for j in range(2):
                for m in range(MEMBERS // 8):
                    rows = swap_groups(
                        [block[m * 8 : m * 8 + 8] for block in updated[4 * j : 4 * j + 4]]
                    )
                    for r in range(BR):
                        at = pl.ds(m * 64 + a * BR + r, 8, stride=8)
                        flat_lines[part, j, at, :] = rows[r]

        for j in range(2):
            out_copy(part, j).start()

    @pl.loop(0, PARTS)
    def _(part):
        for j in range(2):
            out_copy(part, j).wait()

    store_c.wait()


def assimilate(*arguments):
    field = (ROWS, COLS)
    f32 = jnp.float32
    anywhere = pl.BlockSpec(memory_space=pl.ANY)
    local = pl.BlockSpec(memory_space=pltpu.VMEM)
    halo = pltpu.VMEM((STEPS, TILES, OWN, 128), f32)
    dma = pltpu.SemaphoreType.DMA
    square = pltpu.VMEM((BLOCKS, MEMBERS, 128), f32)
    return pl.pallas_call(
        assimilate_kernel,
        out_shape=(
            jax.ShapeDtypeStruct((MEMBERS, ROWS, 2 * 128), f32),
            jax.ShapeDtypeStruct((OWN, ROWS, COLS), f32),
        ),
        in_specs=[anywhere] * 6 + [local] * 4 + [pl.BlockSpec(memory_space=pltpu.SMEM)],
        out_specs=[anywhere] * 2,
        scratch_shapes=[
            *[pltpu.VMEM((TILES + 2, OWN, PAD_ROWS, 128), f32)] * 2,
            *[pltpu.VMEM((OWN, ROWS, COLS), f32)] * 2,
            *[pltpu.VMEM(field, f32)] * 4,
            *[pltpu.VMEM((8, COLS), f32)] * 2,
            *[pltpu.VMEM(field, f32)] * 5,
            *[halo] * 4,
            pltpu.VMEM((PEERS, BLOCKS, OWN, 128), f32),
            pltpu.VMEM((SIDE, 128), jnp.int32),
            *[pltpu.VMEM((SIDE, 128), f32)] * 2,
            pltpu.VMEM((PEERS, SIDE, 128), jnp.int32),
            pltpu.VMEM((PEERS, SIDE, OWN, 128), f32),
            pltpu.VMEM((SIDE, MEMBERS, 128), f32),
            pltpu.VMEM((SIDE + 2, SIDE + 2, 2 * OBS_MAX, 128), f32),
            *[pltpu.VMEM((PAIRS, 2 * HALF, 128), f32)] * 2,
            *[pltpu.VMEM((PAIRS, HALF, 128), f32)] * 3,
            square, square,
            pltpu.VMEM((PARTS, 2, MEMBERS, 8, 128), f32),
            dma((5,)), dma((TILES,)), dma((2,)), dma((2,)),
            dma((STEPS, 2)), dma((STEPS, 2)), dma((PARTS, PEERS)), dma((PARTS, PEERS)),
            dma((2,)), dma,
            dma((PEERS,)), dma((PEERS,)), dma((PEERS,)), dma((PEERS,)), dma((4,)), dma((4,)),
            dma((PARTS, 2)),
        ],
        compiler_params=pltpu.CompilerParams(
            collective_id=0, has_side_effects=True, vmem_limit_bytes=62 << 20
        ),
        name="assimilate",
    )(*arguments)


def on_device(*arguments):
    return assimilate(*arguments[:-1], arguments[-1].transpose(0, 2, 1))


def solution(mesh):
    placed = (
        P("mem", "slab", None),
        P("mem", "slab", None),
        P("slab", None),
        P("slab", None),
        P("slab", None),
        P("slab", None),
        P("slab", "mem", None),
        P("slab", "mem", None),
        P("slab", "mem", None),
        P("slab", "mem"),
        P("slab", "mem", None),
    )
    return jax.shard_map(
        on_device,
        mesh=mesh,
        in_specs=placed,
        out_specs=(P(None, "slab", "mem"), P("mem", "slab", None)),
        check_vma=False,
    )
```

```python
import math

import jax
import jax.numpy as jnp
from jax import lax
from jax.experimental import pallas as pl
from jax.experimental.pallas import tpu as pltpu
from jax.sharding import PartitionSpec as P

MEMBERS = 128
STEPS = 4
BR = 4
BC = 32
OBS_MAX = 16
NBR = 4
NS_ITERS = 7

PEERS = 16
SLABS = 8
OWN = 8
ROWS = 32
COLS = 4096
TILES = 32
PAD_ROWS = 48
BLOCKS = 64
SIDE = 8
PAIRS = 8
PARTS = 4
HALF = NBR * OBS_MAX

inflation = 1.1
ridge = (MEMBERS - 1) / inflation
member_root = math.sqrt(MEMBERS - 1)
side_weight = math.exp(-0.25)
corner_weight = math.exp(-0.5)
mesh_ids = pl.DeviceIdType.MESH

ways = (
    (2, 2), (0, 1), (1, 0), (1, 1), (3, 3), (0, 3), (3, 0), (1, 3), (3, 1), (0, 2), (2, 0),
    (2, 1), (1, 2), (2, 3), (3, 2),
)


def split(value):
    head = value.astype(jnp.bfloat16)
    return head, (value - head.astype(jnp.float32)).astype(jnp.bfloat16)


def product(left, head, tail):
    left_head, left_tail = split(left)
    both = jnp.concatenate([head, tail], axis=1)
    result = jnp.dot(
        jnp.concatenate([left_head, left_tail], axis=1),
        jnp.concatenate([both, both], axis=0),
        preferred_element_type=jnp.float32,
    )
    columns = head.shape[1]
    return result[:, :columns] + result[:, columns:]


def pair_product(left, right):
    same = (lax.broadcasted_iota(jnp.int32, (128, 128), 0) < HALF) == (
        lax.broadcasted_iota(jnp.int32, (128, 128), 1) < HALF
    )
    head, tail = (
        jnp.where(same, jnp.concatenate([part, part], axis=0), jnp.zeros((128, 128), jnp.bfloat16))
        for part in split(right)
    )
    return product(left, head, tail)


def swap_groups(rows):
    group = lax.broadcasted_iota(jnp.int32, (8, 128), 1) // BC
    even = group % 2 == 0
    low = group < 2
    near = [None] * 4
    for i in (0, 2):
        near[i] = jnp.where(even, rows[i], pltpu.roll(rows[i + 1], BC, 1))
        near[i + 1] = jnp.where(even, pltpu.roll(rows[i], 128 - BC, 1), rows[i + 1])
    out = [None] * 4
    for i in (0, 1):
        out[i] = jnp.where(low, near[i], pltpu.roll(near[i + 2], 64, 1))
        out[i + 2] = jnp.where(low, pltpu.roll(near[i], 64, 1), near[i + 2])
    return out


def assimilate_kernel(
    p_in, c_in, d_in, lp_in, lv_in, rate_in, cell_in, value_in, error_in, count_in, neighbour,
    analysis, c_out,
    p, p_other, c, c_other, lp, lv, rate, dif, dif_top, dif_low, keep, k_up, k_down, k_left, k_right,
    out_up, out_down, in_top, in_low, send,
    cells, values, roots, all_cells, obs_send, obs_in, obs_pad,
    rows_z, innov_z, now_x, now_m, now_d, weights_now, gathered, lines,
    load_sem, p_sem, dif_send, dif_recv, halo_send, halo_recv, send_sem, recv_sem, own_sem, c_sem,
    cell_send, cell_recv, obs_send_sem, obs_recv_sem, side_send, side_recv, out_sem,
):
    mem = lax.axis_index("mem")
    slab = lax.axis_index("slab")
    above = lax.rem(slab + SLABS - 1, SLABS)
    below = lax.rem(slab + 1, SLABS)

    def load_p(tile):
        return pltpu.make_async_copy(
            p_in.at[:, :, pl.ds(pl.multiple_of(tile * 128, 128), 128)],
            p.at[tile + 1, :, pl.ds(8, ROWS), :],
            p_sem.at[tile],
        )

    loads = [
        pltpu.make_async_copy(src, dst, load_sem.at[i])
        for i, (src, dst) in enumerate(
            ((d_in, dif), (lp_in, lp), (lv_in, lv), (rate_in, rate), (c_in, c))
        )
    ]
    for load in loads[:-1]:
        load.start()

    @pl.loop(0, TILES)
    def _(tile):
        load_p(tile).start()

    loads[-1].start()

    barrier = pltpu.get_barrier_semaphore()

    @pl.loop(1, PEERS)
    def _(i):
        pl.semaphore_signal(
            barrier, inc=1, device_id=(lax.rem(mem + i, PEERS), slab),
            device_id_type=pl.DeviceIdType.MESH,
        )

    for other in (above, below):
        pl.semaphore_signal(
            barrier, inc=1, device_id=(mem, other), device_id_type=pl.DeviceIdType.MESH
        )

    lane = lax.broadcasted_iota(jnp.int32, (8, 128), 1)
    line = lax.broadcasted_iota(jnp.int32, (8, 128), 0)
    slot_group = lane // OBS_MAX

    def lay_out(piece_of):
        out = piece_of(0)
        for b in range(1, SIDE):
            out = jnp.where(slot_group == b, piece_of(b), out)
        return out

    def slots_of(ref):
        return lay_out(lambda b: jnp.concatenate([ref[:, b, :]] * SIDE, axis=1))

    cells[...] = slots_of(cell_in)
    values[...] = slots_of(value_in)
    counts = lay_out(lambda b: jnp.broadcast_to(count_in[:, b : b + 1], (SIDE, 128)))
    live = lax.rem(lane, OBS_MAX) < counts
    roots[...] = jnp.where(live, jnp.sqrt(slots_of(error_in)), 0.0)

    zero = jnp.zeros((8, 128), jnp.float32)
    for field in (p, p_other):
        for tile in (0, TILES + 1):
            for m in range(OWN):
                for i in range(PAD_ROWS // 8):
                    field[tile, m, i * 8 : i * 8 + 8, :] = zero

    pl.semaphore_wait(barrier, PEERS + 1)

    def dif_copy(i, src, dst, other):
        return pltpu.make_async_remote_copy(
            src_ref=src, dst_ref=dst, send_sem=dif_send.at[i], recv_sem=dif_recv.at[i],
            device_id=(mem, other), device_id_type=pl.DeviceIdType.MESH,
        )

    def cell_copy(i):
        return pltpu.make_async_remote_copy(
            src_ref=cells, dst_ref=all_cells.at[mem],
            send_sem=cell_send.at[i], recv_sem=cell_recv.at[i],
            device_id=(lax.rem(mem + i, PEERS), slab), device_id_type=mesh_ids,
        )

    @pl.loop(1, PEERS)
    def _(i):
        cell_copy(i).start()

    all_cells[mem] = cells[...]

    dif_copies = [
        dif_copy(0, d_in.at[pl.ds(24, 8)], dif_top, below),
        dif_copy(1, d_in.at[pl.ds(0, 8)], dif_low, above),
    ]
    for copy in dif_copies:
        copy.start()

    def halo_copy(step, i):
        src, dst, other = ((out_down, in_top, below), (out_up, in_low, above))[i]
        return pltpu.make_async_remote_copy(
            src_ref=src.at[step], dst_ref=dst.at[step],
            send_sem=halo_send.at[step, i], recv_sem=halo_recv.at[step, i],
            device_id=(mem, other), device_id_type=pl.DeviceIdType.MESH,
        )

    flat, flat_other = (
        field.reshape(TILES + 2, OWN * PAD_ROWS, 128) for field in (p, p_other)
    )

    def send_halo(step):
        for i in range(2):
            halo_copy(step, i).start()

    first_row = pl.ds(8, OWN, stride=PAD_ROWS)
    last_row = pl.ds(7 + ROWS, OWN, stride=PAD_ROWS)

    def clear_outside(field, tile):
        field[tile + 1, pl.ds(7, OWN, stride=PAD_ROWS), :] = zero
        field[tile + 1, pl.ds(8 + ROWS, OWN, stride=PAD_ROWS), :] = zero

    @pl.loop(0, TILES, unroll=8)
    def _(tile):
        clear_outside(flat_other, tile)

    for load in loads[:-1]:
        load.wait()
    for copy in dif_copies:
        copy.wait()

    first, last = lane == 0, lane == 127
    at_top, at_low = slab == 0, slab == SLABS - 1

    @pl.loop(0, TILES, unroll=4)
    def _(tile):
        here = pl.ds(pl.multiple_of(tile * 128, 128), 128)
        left = pl.ds(pl.multiple_of(jnp.maximum(tile - 1, 0) * 128, 128), 128)
        right = pl.ds(pl.multiple_of(jnp.minimum(tile + 1, TILES - 1) * 128, 128), 128)
        top_row = jnp.where(at_top, 0.0, dif_top[:, here])
        low_row = jnp.where(at_low, 0.0, dif_low[:, here])
        mids = [dif[i * 8 : i * 8 + 8, here] for i in range(4)]
        column = [top_row, *mids, low_row]
        for i in range(4):
            rows = slice(i * 8, i * 8 + 8)
            mid = mids[i]
            up = jnp.where(line == 0, pltpu.roll(column[i], 1, 0), pltpu.roll(mid, 1, 0))
            down = jnp.where(line == 7, pltpu.roll(column[i + 2], 7, 0), pltpu.roll(mid, 7, 0))
            next_left = jnp.where(tile == 0, 0.0, dif[rows, left])
            next_right = jnp.where(tile == TILES - 1, 0.0, dif[rows, right])
            west = jnp.where(first, pltpu.roll(next_left, 1, 1), pltpu.roll(mid, 1, 1))
            east = jnp.where(last, pltpu.roll(next_right, 127, 1), pltpu.roll(mid, 127, 1))
            sides = [0.1 * (mid + side) for side in (up, down, west, east)]
            for ref, side in zip((k_up, k_down, k_left, k_right), sides):
                ref[rows, here] = side
            keep[rows, here] = 1.0 - ((sides[0] + sides[1]) + (sides[2] + sides[3]))
            lv[rows, here] = lv[rows, here] * rate[rows, here]

    @pl.loop(0, TILES)
    def _(tile):
        load_p(tile).wait()

    @pl.loop(0, TILES, unroll=8)
    def _(tile):
        clear_outside(flat, tile)
        out_up[0, tile] = flat[tile + 1, first_row, :]
        out_down[0, tile] = flat[tile + 1, last_row, :]

    send_halo(0)

    loads[-1].wait()

    wide = 4

    def advance(now, content_now, later, content_later):

        @pl.loop(0, TILES // wide)
        def _(group):
            for row_tile in range(ROWS // 8):
                rows = slice(row_tile * 8, row_tile * 8 + 8)
                base = 8 + row_tile * 8
                heres = [
                    pl.ds(pl.multiple_of((group * wide + j) * 128, 128), 128) for j in range(wide)
                ]
                weights = [
                    [ref[rows, here] for ref in (keep, k_up, k_down, k_left, k_right, lp, lv, rate)]
                    for here in heres
                ]
                for m in range(OWN):
                    mids = [
                        now[group * wide + j, m, base : base + 8, :] for j in range(wide + 2)
                    ]
                    to_right = [pltpu.roll(mids[j], 1, 1) for j in range(wide + 1)]
                    to_left = [None] + [pltpu.roll(mids[j], 127, 1) for j in range(1, wide + 2)]
                    for j in range(wide):
                        keep_w, up_w, down_w, left_w, right_w, lp_w, lv_w, rate_w = weights[j]
                        tile = group * wide + j + 1
                        mid = mids[j + 1]
                        up = now[tile, m, base - 1 : base + 7, :]
                        down = now[tile, m, base + 1 : base + 9, :]
                        west = jnp.where(first, to_right[j], to_right[j + 1])
                        east = jnp.where(last, to_left[j + 2], to_left[j + 1])
                        content = content_now[m, rows, heres[j]]
                        inverse = pltpu.reciprocal(lp_w + jnp.abs(mid), approx=True)
                        release = rate_w * content - (lv_w * mid) * inverse
                        flow = (up_w * up + down_w * down) + (left_w * west + right_w * east)
                        later[tile, m, base : base + 8, :] = (
                            keep_w * mid + flow + release
                        )
                        content_later[m, rows, heres[j]] = content - release

    def one_step(step, now, content_now, later, content_later, flat_later, more):
        advance(now, content_now, later, content_later)
        for i in range(2):
            halo_copy(step, i).wait()
        following = lax.rem(step + 1, STEPS)

        @pl.loop(0, TILES, unroll=8)
        def _(tile):
            here = pl.ds(pl.multiple_of(tile * 128, 128), 128)
            top = jnp.where(at_top, 0.0, in_top[step, tile]) * k_up[0:1, here]
            low = jnp.where(at_low, 0.0, in_low[step, tile]) * k_down[ROWS - 1 : ROWS, here]
            top = flat_later[tile + 1, first_row, :] + top
            low = flat_later[tile + 1, last_row, :] + low
            flat_later[tile + 1, first_row, :] = top
            flat_later[tile + 1, last_row, :] = low
            out_up[following, tile] = top
            out_down[following, tile] = low

        @pl.when(more)
        def _():
            send_halo(step + 1)

    @pl.loop(0, STEPS // 2)
    def _(pair):
        one_step(2 * pair, p, c, p_other, c_other, flat_other, True)
        one_step(2 * pair + 1, p_other, c_other, p, c, flat, pair < STEPS // 2 - 1)

    store_c = pltpu.make_async_copy(c, c_out, c_sem)
    store_c.start()

    @pl.loop(1, PEERS)
    def _(i):
        cell_copy(i).wait()

    def to_blocks(target):
        for a in range(SIDE):
            index = jnp.broadcast_to(all_cells[target, a : a + 1, :], (OWN, 128))
            observed = jnp.zeros((OWN, 128), jnp.float32)
            for j in range(2):
                lines = [
                    flat[target * 2 + j + 1, pl.ds(8 + a * BR + r, OWN, stride=PAD_ROWS), :]
                    for r in range(BR)
                ]
                blocks = swap_groups(lines)
                for b in range(4):
                    send[target, a * SIDE + j * 4 + b] = blocks[b]
                    picked = jnp.take_along_axis(blocks[b], index, axis=1)
                    observed = jnp.where(slot_group == j * 4 + b, picked, observed)
            obs_send[target, a] = observed

    mine = pl.ds(pl.multiple_of(mem * OWN, OWN), OWN)

    def place_of(code):
        return lax.rem(mem // 4 + code // 4, 4) * 4 + lax.rem(mem + code, 4)

    def obs_copy(i):
        target = place_of(i)
        return pltpu.make_async_remote_copy(
            src_ref=obs_send.at[target], dst_ref=obs_in.at[:, mine, :],
            send_sem=obs_send_sem.at[i], recv_sem=obs_recv_sem.at[i],
            device_id=(target, slab), device_id_type=mesh_ids,
        )

    def block_copy(part, i):
        target = place_of(i)
        blocks = pl.ds(part * 2 * SIDE, 2 * SIDE)
        return pltpu.make_async_remote_copy(
            src_ref=send.at[target, blocks], dst_ref=gathered.at[blocks, mine, :],
            send_sem=send_sem.at[part, i], recv_sem=recv_sem.at[part, i],
            device_id=(target, slab), device_id_type=mesh_ids,
        )

    @pl.loop(1, PEERS)
    def _(i):
        code = lax.rem(7 * i, PEERS)
        to_blocks(place_of(code))
        obs_copy(code).start()
        block_copy(0, code).start()

    to_blocks(mem)
    own = pltpu.make_async_copy(send.at[mem], gathered.at[:, mine, :], own_sem.at[0])
    own.start()
    own_obs = pltpu.make_async_copy(obs_send.at[mem], obs_in.at[:, mine, :], own_sem.at[1])
    own_obs.start()
    own_obs.wait()

    @pl.loop(1, PEERS)
    def _(i):
        obs_copy(i).wait()

    @pl.loop(0, SIDE)
    def _(a):
        seen = obs_in[a]
        centre = jnp.mean(seen, axis=0, keepdims=True)
        root = roots[pl.ds(a, 1), :]
        spread = ((seen - centre) * root).T
        innovation = jnp.broadcast_to((values[pl.ds(a, 1), :] - centre) * root, (128, 128)).T
        for b in range(SIDE):
            obs_pad[a + 1, b + 1, 0:OBS_MAX, :] = spread[b * OBS_MAX : (b + 1) * OBS_MAX]
            obs_pad[a + 1, b + 1, OBS_MAX:, :] = innovation[b * OBS_MAX : (b + 1) * OBS_MAX]

    def side_copy(i):
        src, dst, device = (
            (obs_pad.at[1:9, 8], obs_pad.at[1:9, 0], (lax.rem(mem + 1, PEERS), slab)),
            (obs_pad.at[1:9, 1], obs_pad.at[1:9, 9], (lax.rem(mem + PEERS - 1, PEERS), slab)),
            (obs_pad.at[8], obs_pad.at[0], (mem, below)),
            (obs_pad.at[1], obs_pad.at[9], (mem, above)),
        )[i]
        return pltpu.make_async_remote_copy(
            src_ref=src, dst_ref=dst, send_sem=side_send.at[i], recv_sem=side_recv.at[i],
            device_id=device, device_id_type=mesh_ids,
        )

    blank = jnp.zeros((2 * OBS_MAX, 128), jnp.float32)
    for sides, conditions in (
        ((0, 1), (mem == 0, mem == PEERS - 1)),
        ((2, 3), (at_top, at_low)),
    ):
        for i in sides:
            side_copy(i).start()
        for i in sides:
            side_copy(i).wait()
        if sides[0] == 0:

            @pl.loop(1, PARTS)
            def _(part):
                for way in ways:
                    block_copy(part, 4 * way[0] + way[1]).start()

        for i, condition in zip(sides, conditions):

            @pl.when(condition)
            def _(i=i):
                @pl.loop(*((1, SIDE + 1) if i < 2 else (0, SIDE + 2)))
                def _(place):
                    if i < 2:
                        obs_pad[place, 0 if i == 0 else SIDE + 1] = blank
                    else:
                        obs_pad[0 if i == 2 else SIDE + 1, place] = blank

    half_lane = lax.broadcasted_iota(jnp.int32, (1, 128), 1) < HALF
    diagonal = lax.broadcasted_iota(jnp.int32, (HALF, 128), 0) == lax.rem(
        lax.broadcasted_iota(jnp.int32, (HALF, 128), 1), HALF
    )
    pair_eye = jnp.where(diagonal, 1.0, 0.0)
    eye = lax.broadcasted_iota(jnp.int32, (128, 128), 0) == lax.broadcasted_iota(
        jnp.int32, (128, 128), 1
    )
    no_rows = jnp.zeros((HALF, 128), jnp.float32)

    @pl.loop(0, BLOCKS // (2 * PAIRS))
    def _(group):
        start = []
        for pair in range(PAIRS):
            for i in range(2 * NBR):
                place = 2 * pair + i // NBR
                a = group * (PAIRS // 4) + place // SIDE
                b = place % SIDE
                code = neighbour[a, i % NBR, b]
                down_by = lax.div(code, 3)
                right_by = code - 3 * down_by
                block = obs_pad[a + down_by, b + right_by]
                far = (down_by != 1).astype(jnp.int32) + (right_by != 1).astype(jnp.int32)
                weight = jnp.where(
                    far == 0, 1.0, jnp.where(far == 1, side_weight, corner_weight)
                )
                rows_z[pair, i * OBS_MAX : (i + 1) * OBS_MAX, :] = weight * block[:OBS_MAX]
                innov_z[pair, i * OBS_MAX : (i + 1) * OBS_MAX, :] = weight * block[OBS_MAX:]
        rows = [rows_z[pair] for pair in range(PAIRS)]
        grams = [product(z, *split(z.T)) for z in rows]
        smalls = [jnp.where(half_lane, gram[:HALF], gram[HALF:]) for gram in grams]
        traces = [
            jnp.sum(jnp.where(diagonal, small, 0.0), axis=0, keepdims=True) for small in smalls
        ]
        totals = [
            [
                MEMBERS * ridge + jnp.sum(jnp.where(side, trace, 0.0), axis=1, keepdims=True)
                for side in (half_lane, jnp.logical_not(half_lane))
            ]
            for trace in traces
        ]
        for pair, (small, total) in enumerate(zip(smalls, totals)):
            scale = 1.0 / jnp.where(half_lane, total[0], total[1])
            low = ridge * scale
            now_x[pair] = small * scale + low * pair_eye
            now_m[pair] = no_rows
            now_d[pair] = pair_eye
            start.append((low, jnp.ones_like(low)))

        def sweep(_, carry):
            states = [(now_x[i], now_m[i], now_d[i]) for i in range(PAIRS)]
            by_x = [
                pair_product(jnp.concatenate(state, axis=0), state[0]) for state in states
            ]
            factors = [
                0.25 * result[:HALF] - 1.5 * state[0] + 2.25 * pair_eye
                for result, state in zip(by_x, states)
            ]
            by_f = [
                pair_product(jnp.concatenate([x, d], axis=0), factor)
                for (x, _, d), factor in zip(states, factors)
            ]
            ahead = []
            later = []
            for (x, m, d), (low, gain), first, second in zip(states, carry, by_x, by_f):
                new_d = (
                    second[HALF:]
                    + (0.25 * low) * first[2 * HALF :]
                    + (0.25 * low * (low - 6.0)) * d
                )
                new_m = 1.5 * m - 0.5 * first[HALF : 2 * HALF] - (0.5 * gain) * d
                later.append((second[:HALF], new_m, new_d))
                shrink = 1.5 - 0.5 * low
                ahead.append((low * shrink * shrink, gain * shrink))
            for i in range(PAIRS):
                now_x[i], now_m[i], now_d[i] = later[i]
            return tuple(ahead)

        last_low = lax.fori_loop(0, NS_ITERS - 1, sweep, tuple(start))
        states = [(now_x[i], now_m[i], now_d[i]) for i in range(PAIRS)]
        rows = [rows_z[pair] for pair in range(PAIRS)]
        by_x = [pair_product(m, x) for x, m, _ in states]
        ends = []
        for (_, m, d), (_, gain), total, result in zip(states, last_low, totals, by_x):
            both = jnp.where(half_lane, total[0], total[1])
            m = 1.5 * m - 0.5 * result - (0.5 * gain) * d
            m = m * (1.0 / (both * jnp.sqrt(both)))
            ends.append(
                jnp.concatenate(
                    [jnp.where(half_lane, m, 0.0), jnp.where(half_lane, 0.0, m)], axis=0
                )
            )
        by_z = [product(end, *split(z)) for end, z in zip(ends, rows)]
        wide_z = [
            jnp.concatenate(
                [
                    jnp.concatenate([m_z[:HALF], no_rows], axis=0),
                    jnp.concatenate([no_rows, m_z[HALF:]], axis=0),
                ],
                axis=1,
            )
            for m_z in by_z
        ]
        roots_both = [product(z.T, *split(right)) for z, right in zip(rows, wide_z)]
        gains = []
        pulls = []
        for pair, (z, total) in enumerate(zip(rows, totals)):
            for side in range(2):
                low = ridge / total[side]
                gain = 1.0 / jnp.sqrt(total[side])
                for _ in range(NS_ITERS):
                    shrink = 1.5 - 0.5 * low
                    low, gain = low * shrink * shrink, gain * shrink
                gains.append(gain)
                own_rows = slice(side * HALF, side * HALF + HALF)
                pulls.append(
                    jnp.sum(innov_z[pair, own_rows] * z[own_rows], axis=0, keepdims=True)
                )
        for i, (gain, pull) in enumerate(zip(gains, pulls)):
            column = i % 2 * 128
            root = roots_both[i // 2][:, column : column + 128] + jnp.where(eye, gain, 0.0)
            first_pass = jnp.sum(root * pull, axis=1, keepdims=True)
            shift = jnp.sum(root * first_pass, axis=0, keepdims=True)
            weights_now[group * 2 * PAIRS + i] = member_root * root + shift

    flat_lines = lines.reshape(PARTS, 2, MEMBERS * 8, 128)

    def out_copy(part, j):
        return pltpu.make_async_copy(
            lines.at[part, j],
            analysis.at[:, pl.ds(pl.multiple_of(part * 8, 8), 8), pl.ds(j * 128, 128)],
            out_sem.at[part, j],
        )

    own.wait()

    @pl.loop(0, PARTS)
    def _(part):
        @pl.loop(1, PEERS)
        def _(i):
            block_copy(part, i).wait()

        @pl.loop(0, 2)
        def _(a):
            places = [part * 2 * SIDE + a * SIDE + b for b in range(SIDE)]
            fields = [gathered[place] for place in places]
            centres = [jnp.mean(field, axis=0, keepdims=True) for field in fields]
            updated = [
                product(weights_now[place], *split(field - centre)) + centre
                for place, field, centre in zip(places, fields, centres)
            ]
            for j in range(2):
                for m in range(MEMBERS // 8):
                    rows = swap_groups(
                        [block[m * 8 : m * 8 + 8] for block in updated[4 * j : 4 * j + 4]]
                    )
                    for r in range(BR):
                        at = pl.ds(m * 64 + a * BR + r, 8, stride=8)
                        flat_lines[part, j, at, :] = rows[r]

        for j in range(2):
            out_copy(part, j).start()

    @pl.loop(0, PARTS)
    def _(part):
        for j in range(2):
            out_copy(part, j).wait()

    store_c.wait()


def assimilate(*arguments):
    field = (ROWS, COLS)
    f32 = jnp.float32
    anywhere = pl.BlockSpec(memory_space=pl.ANY)
    local = pl.BlockSpec(memory_space=pltpu.VMEM)
    halo = pltpu.VMEM((STEPS, TILES, OWN, 128), f32)
    dma = pltpu.SemaphoreType.DMA
    square = pltpu.VMEM((BLOCKS, MEMBERS, 128), f32)
    return pl.pallas_call(
        assimilate_kernel,
        out_shape=(
            jax.ShapeDtypeStruct((MEMBERS, ROWS, 2 * 128), f32),
            jax.ShapeDtypeStruct((OWN, ROWS, COLS), f32),
        ),
        in_specs=[anywhere] * 6 + [local] * 4 + [pl.BlockSpec(memory_space=pltpu.SMEM)],
        out_specs=[anywhere] * 2,
        scratch_shapes=[
            *[pltpu.VMEM((TILES + 2, OWN, PAD_ROWS, 128), f32)] * 2,
            *[pltpu.VMEM((OWN, ROWS, COLS), f32)] * 2,
            *[pltpu.VMEM(field, f32)] * 4,
            *[pltpu.VMEM((8, COLS), f32)] * 2,
            *[pltpu.VMEM(field, f32)] * 5,
            *[halo] * 4,
            pltpu.VMEM((PEERS, BLOCKS, OWN, 128), f32),
            pltpu.VMEM((SIDE, 128), jnp.int32),
            *[pltpu.VMEM((SIDE, 128), f32)] * 2,
            pltpu.VMEM((PEERS, SIDE, 128), jnp.int32),
            pltpu.VMEM((PEERS, SIDE, OWN, 128), f32),
            pltpu.VMEM((SIDE, MEMBERS, 128), f32),
            pltpu.VMEM((SIDE + 2, SIDE + 2, 2 * OBS_MAX, 128), f32),
            *[pltpu.VMEM((PAIRS, 2 * HALF, 128), f32)] * 2,
            *[pltpu.VMEM((PAIRS, HALF, 128), f32)] * 3,
            square, square,
            pltpu.VMEM((PARTS, 2, MEMBERS, 8, 128), f32),
            dma((5,)), dma((TILES,)), dma((2,)), dma((2,)),
            dma((STEPS, 2)), dma((STEPS, 2)), dma((PARTS, PEERS)), dma((PARTS, PEERS)),
            dma((2,)), dma,
            dma((PEERS,)), dma((PEERS,)), dma((PEERS,)), dma((PEERS,)), dma((4,)), dma((4,)),
            dma((PARTS, 2)),
        ],
        compiler_params=pltpu.CompilerParams(
            collective_id=0, has_side_effects=True, vmem_limit_bytes=62 << 20
        ),
        name="assimilate",
    )(*arguments)


def on_device(*arguments):
    return assimilate(*arguments[:-1], arguments[-1].transpose(0, 2, 1))


def solution(mesh):
    placed = (
        P("mem", "slab", None),
        P("mem", "slab", None),
        P("slab", None),
        P("slab", None),
        P("slab", None),
        P("slab", None),
        P("slab", "mem", None),
        P("slab", "mem", None),
        P("slab", "mem", None),
        P("slab", "mem"),
        P("slab", "mem", None),
    )
    return jax.shard_map(
        on_device,
        mesh=mesh,
        in_specs=placed,
        out_specs=(P(None, "slab", "mem"), P("mem", "slab", None)),
        check_vma=False,
    )
```
